128 devices in a mesh: ctx: 8 (over z_lo, x), exp: 16 (over z_hi, y, core).
Axes of the slice: x: 4, y: 4, z: 4 (z_hi: 2, z_lo: 2; z = z_hi * 2 + z_lo), core: 2. Of those that a mesh axis runs over, the one named last changes fastest.
Arguments:
- hidden_in: bfloat16 [16384, 2880], P(('ctx', 'exp')), may hold values from -6 to 6
- query_proj: bfloat16 [16384, 2048], P(('ctx', 'exp')), may hold values from -120 to 120
- key_proj: bfloat16 [16384, 256], P(('ctx', 'exp')), may hold values from -4 to 4
- value_proj: bfloat16 [16384, 256], P(('ctx', 'exp')), may hold values from -6 to 6
- sink_logits: float32 [32], replicated, may hold values from 0 to 4
- out_weight: bfloat16 [2048, 2880], P('exp'), may hold values from -0.125 to 0.125
- norm_gain: float32 [2880], replicated, may hold values from 0.1 to 1.9
- expert_ids: int32 [16384, 4], P(('ctx', 'exp')), may hold values from 0 to 63, all different within a row; in each aligned block of 128 rows (0 to 127, 128 to 255, ...) at most 8 rows name the same one
- gate_weights: float32 [16384, 4], P(('ctx', 'exp')), may hold values from 0.1 to 0.5
- gate_proj: bfloat16 [128, 2880, 720], P(('ctx', 'exp')), may hold values from -0.109375 to 0.109375
- up_proj: bfloat16 [128, 2880, 720], P(('ctx', 'exp')), may hold values from -0.109375 to 0.109375
- down_proj: bfloat16 [128, 720, 2880], P(('ctx', 'exp')), may hold values from -0.15625 to 0.15625
- out_grad: bfloat16 [16384, 2880], P(('ctx', 'exp')), may hold values from -6 to 6
Outputs:
- layer_out: bfloat16 [16384, 2880], P(('ctx', 'exp'))
- resid_grad: bfloat16 [16384, 2880], P(('ctx', 'exp'))
- query_grad: bfloat16 [16384, 2048], P(('ctx', 'exp'))
- key_grad: bfloat16 [16384, 256], P(('ctx', 'exp'))
- value_grad: bfloat16 [16384, 256], P(('ctx', 'exp'))
The draws below stay inside these ranges and needn't reach their ends.
Inputs may be any that keep to these rules, and one draw needn't show every extreme that they name: `expert_ids`: each row names 4 different experts; within the rows of one device (aligned blocks of 128 rows) every expert is named by exactly 8 rows.
All inputs are finite; a program needn't handle non-finite values.
Results may differ from the reference program's by a relative error of at most 0.017.
Values may be sent and summed in bfloat16 or wider, within the bound.
No kernel may reach another device: no remote copies, remote signals or barrier semaphores. Data moves between devices by JAX's collectives and lax.ppermute only.
A program may use at most 192 MiB of HBM per device.

```python
import math
import jax
import jax.numpy as jnp
import numpy as np
from jax import lax

D = 2880
HQ = 32
KVH = 4
DH = 64
FF = 1440
TOPK = 4
WINDOW = 128
TOK_DEV = 128
HALF = 720
SEQ = 16384
EXPERTS = 64
CAP = 8


def common_keys(key):
    return jnp.clip(jax.random.normal(key, (SEQ, KVH, DH), jnp.float32), -4.0, 4.0)


def draw_key_proj(key, part):
    base = common_keys(key)
    return base.reshape(SEQ, KVH * DH).astype(jnp.bfloat16)


def draw_query_proj(key, part):
    key = jax.random.fold_in(key, 5)
    own = jnp.clip(2.0 * jax.random.normal(key, (SEQ, HQ, DH), jnp.float32), -8.0, 8.0)
    return own.reshape(SEQ, HQ * DH).astype(jnp.bfloat16)


def shard_levels(stream_key, shape, pieces, smallest, high):
    gain, own = 1.0, jax.random.fold_in(stream_key, 6)
    for dim, parts in pieces:
        heights = jnp.exp(jax.random.uniform(jax.random.fold_in(own, dim), (parts,), jnp.float32, smallest / len(pieces), high / len(pieces)))
        gain = gain * jnp.repeat(heights, shape[dim] // parts).reshape([-1 if axis == dim else 1 for axis in range(len(shape))])
    return gain


def shared_out(own_key, own, number, rows, count, top, bound, lean):
    ranking = jax.random.permutation(own_key, count)
    crowded, ordinary = portions_of(count, rows * top, bound, lean, True), portions_of(count, rows * top, bound, lean, False)
    places = jnp.arange(count)

    def named(tallies, offset_by):
        used = int((tallies > 0).sum())
        fixed = max(1, used // 4)
        shifted = fixed + (places - fixed + offset_by * (used - fixed)) % max(1, count - fixed)
        return jnp.zeros((count,), jnp.int32).at[ranking[jnp.where(places < fixed, places, shifted)]].set(jnp.asarray(tallies, jnp.int32))

    tallies = jnp.where(number % 4 == 0, named(crowded, number // 4), named(ordinary, number - number // 4 - 1))
    mixed = jax.random.permutation(jax.random.fold_in(own, 3), count)
    giver, receiver = mixed[0:count // 2 * 2:2], mixed[1:count // 2 * 2:2]
    margin = jnp.minimum(tallies[giver] - 1, bound - tallies[receiver]) // 2
    margin = jnp.where((giver == ranking[0]) | (receiver == ranking[0]) | (tallies[receiver] == 0), 0, jnp.maximum(margin, 0))
    shifted = jax.random.randint(jax.random.fold_in(own, 4), (count // 2,), 0, 1 << 20) % (margin + 1)
    tallies = tallies.at[giver].add(-shifted).at[receiver].add(shifted)
    items = jnp.searchsorted(jnp.cumsum(tallies), jnp.arange(rows * top), side="right").astype(jnp.int32)
    listing = items.reshape(top, rows).T
    listing = listing[jax.random.permutation(jax.random.fold_in(own, 1), rows)]
    offset_by = jax.random.randint(jax.random.fold_in(own, 2), (rows, 1), 0, top)
    return jnp.take_along_axis(listing, (jnp.arange(top)[None, :] + offset_by) % top, axis=1)


def portions_of(count, total, bound, lean, full):
    weights = [(1 << 20) // math.isqrt(standing ** lean) + 1 for standing in range(1, count + 1)]
    largest = bound if full else min(bound, max(-(-total // count), total * weights[0] // sum(weights)))
    least = 1 if total - largest >= count - 1 else 0
    counts, rest = [largest] + [least] * (count - 1), total - largest - least * (count - 1)
    while rest > 0:
        movable = [i for i in range(1, count) if counts[i] < largest] or [i for i in range(1, count) if counts[i] < bound]
        whole, left = sum([weights[i] for i in movable]), rest
        for i in movable:
            more = min(bound - counts[i], max(1, left * weights[i] // whole), rest)
            counts[i] = counts[i] + more
            rest = rest - more
    return np.array(counts)


def gaussian(stream_key, shape, scale, reach, cuts=(), kind=jnp.bfloat16):
    loudness = shard_levels(stream_key, shape, cuts, -0.22, 0.18) if cuts else 1.0
    array = jax.random.normal(stream_key, shape, jnp.float32) * scale * loudness
    return jnp.minimum(jnp.maximum(array, -reach), reach).astype(kind)


def setup_inputs(seed: int = 0) -> dict:
    streams_of = jax.random.split(jax.random.key(seed), 14)
    hidden_in = gaussian(streams_of[0], (SEQ, D), 1.0, 6.0, ((0, 128),))
    query_proj = draw_query_proj(jax.random.fold_in(streams_of[13], 71), 0)
    key_proj = draw_key_proj(jax.random.fold_in(streams_of[13], 71), 0)
    value_proj = gaussian(streams_of[3], (SEQ, KVH * DH), 1.0, 6.0, ((0, 128),))
    sink_logits = jnp.clip(jax.random.uniform(streams_of[4], (HQ,), jnp.float32, 0.0, 4.0), 0.0, 4.0)
    out_weight = gaussian(streams_of[5], (HQ * DH, D), (HQ * DH) ** -0.5, 0.125, ((0, 16),))
    norm_gain = jnp.clip(1.0 + 0.18 * jax.random.normal(streams_of[6], (D,), jnp.float32), 0.1, 1.9)
    expert_ids_keys = jax.random.split(jax.random.fold_in(streams_of[7], 1), SEQ // TOK_DEV)
    expert_ids_turns = jax.random.permutation(jax.random.fold_in(streams_of[7], 3), SEQ // TOK_DEV)
    expert_ids = jax.vmap(lambda own, number: shared_out(jax.random.fold_in(streams_of[7], 2), own, number, TOK_DEV, EXPERTS, TOPK, CAP, 0))(expert_ids_keys, expert_ids_turns).reshape((SEQ, TOPK))
    gate_weights = jnp.clip(0.1 + 0.4 * jax.random.uniform(streams_of[8], (SEQ, TOPK), jnp.float32) ** shard_levels(streams_of[8], (SEQ, TOPK), ((0, 128),), -0.2, 0.2), 0.1, 0.5)
    gate_proj = gaussian(streams_of[9], (2 * EXPERTS, D, HALF), D ** -0.5, 0.109375, ((0, 128),))
    up_proj = gaussian(streams_of[10], (2 * EXPERTS, D, HALF), D ** -0.5, 0.109375, ((0, 128),))
    down_proj = gaussian(streams_of[11], (2 * EXPERTS, HALF, D), FF ** -0.5, 0.15625, ((0, 128),))
    out_grad = gaussian(streams_of[12], (SEQ, D), 1.0, 6.0, ((0, 128),))
    return {"hidden_in": hidden_in, "query_proj": query_proj, "key_proj": key_proj, "value_proj": value_proj, "sink_logits": sink_logits, "out_weight": out_weight, "norm_gain": norm_gain, "expert_ids": expert_ids, "gate_weights": gate_weights, "gate_proj": gate_proj, "up_proj": up_proj, "down_proj": down_proj, "out_grad": out_grad}


NEG = -1e+30
EPS = 1e-05
ALPHA = 1.702

def band_mask(first, count):
    query_pos = first + jnp.arange(count, dtype=jnp.int32)
    key_pos = first - WINDOW + jnp.arange(count + WINDOW, dtype=jnp.int32)
    diff = query_pos[:, None] - key_pos[None, :]
    return (diff >= 0) & (diff < WINDOW) & (key_pos[None, :] >= 0)

def slot_targets(ids):
    flat = ids.reshape(-1)
    table = jnp.arange(EXPERTS, dtype=jnp.int32)
    hits = (flat[:, None] == table[None, :]).astype(jnp.int32)
    before = jnp.cumsum(hits, axis=0) - hits
    slot = lax.optimization_barrier(jnp.sum(before * hits, axis=1))
    return (flat * CAP + slot).reshape(ids.shape).astype(jnp.int32)

def reference(hidden_in, query_proj, key_proj, value_proj, sink_logits, out_weight, norm_gain, expert_ids, gate_weights, gate_proj, up_proj, down_proj, out_grad):
    group = HQ // KVH
    scale = DH ** (-0.5)
    stride = min(512, SEQ)
    starts = jnp.arange(SEQ // stride, dtype=jnp.int32) * stride
    queries = query_proj.reshape(SEQ, HQ, DH).transpose(1, 0, 2)
    padding = jnp.zeros((KVH, WINDOW, DH), jnp.bfloat16)
    keys = jnp.concatenate([padding, key_proj.reshape(SEQ, KVH, DH).transpose(1, 0, 2)], axis=1)
    values = jnp.concatenate([padding, value_proj.reshape(SEQ, KVH, DH).transpose(1, 0, 2)], axis=1)
    heads = jnp.arange(HQ, dtype=jnp.int32)

    def scores_of(q_rows, key_span, start):
        s = jnp.dot(q_rows, key_span.T, preferred_element_type=jnp.float32) * scale
        return jnp.where(band_mask(start, stride), s, NEG)

    def head_forward(item):
        q_head, sink, head = item
        k_head = lax.dynamic_index_in_dim(keys, head // group, 0, keepdims=False)
        v_head = lax.dynamic_index_in_dim(values, head // group, 0, keepdims=False)

        def span_forward(start):
            q_rows = lax.dynamic_slice_in_dim(q_head, start, stride, 0)
            key_span = lax.dynamic_slice_in_dim(k_head, start, stride + WINDOW, 0)
            value_rows = lax.dynamic_slice_in_dim(v_head, start, stride + WINDOW, 0)
            s = scores_of(q_rows, key_span, start)
            peak = jnp.maximum(lax.optimization_barrier(jnp.max(s, axis=1)), sink)
            weights = jnp.exp(s - peak[:, None])
            total = lax.optimization_barrier(jnp.sum(weights, axis=1)) + jnp.exp(sink - peak)
            o = jnp.dot(weights.astype(jnp.bfloat16), value_rows, preferred_element_type=jnp.float32) / total[:, None]
            return (o, peak, total)
        o, peak, total = lax.map(span_forward, starts)
        return (o.reshape(SEQ, DH), peak.reshape(SEQ), total.reshape(SEQ))
    outs, peaks, totals = lax.map(head_forward, (queries, sink_logits, heads))
    attn = outs.transpose(1, 0, 2).reshape(SEQ, HQ * DH).astype(jnp.bfloat16)
    attn_out = jnp.dot(attn, out_weight, preferred_element_type=jnp.float32)
    resid = lax.optimization_barrier((hidden_in.astype(jnp.float32) + attn_out).astype(jnp.bfloat16))
    resid_f = resid.astype(jnp.float32)
    inv_rms = lax.rsqrt(lax.optimization_barrier(jnp.mean(resid_f * resid_f, axis=1, keepdims=True)) + EPS)
    normed = (resid_f * inv_rms * norm_gain).astype(jnp.bfloat16)
    blocks = SEQ // TOK_DEV
    targets = jax.vmap(slot_targets)(expert_ids.reshape(blocks, TOK_DEV, TOPK))
    block_ids = jnp.arange(blocks, dtype=jnp.int32)[:, None, None]
    w_gate = gate_proj.reshape(EXPERTS, 2, D, HALF)
    w_up = up_proj.reshape(EXPERTS, 2, D, HALF)
    w_down = down_proj.reshape(EXPERTS, 2, HALF, D)

    def to_slots(per_pick):
        buf = jnp.zeros((blocks, EXPERTS * CAP, D), per_pick.dtype)
        buf = buf.at[block_ids, targets].set(per_pick)
        return buf.reshape(blocks, EXPERTS, CAP, D).transpose(1, 0, 2, 3).reshape(EXPERTS, blocks * CAP, D)

    def from_slots(per_expert):
        buf = per_expert.reshape(EXPERTS, blocks, CAP, D).transpose(1, 0, 2, 3).reshape(blocks, EXPERTS * CAP, D)
        return buf[block_ids, targets]
    picked_rows = jnp.broadcast_to(normed.reshape(blocks, TOK_DEV, 1, D), (blocks, TOK_DEV, TOPK, D))
    slot_rows = to_slots(picked_rows)

    def expert_forward(item):
        rows_e, gate_e, up_e, down_e = item
        summed = jnp.zeros((rows_e.shape[0], D), jnp.float32)
        for half in range(2):
            gate_act = jnp.dot(rows_e, gate_e[half], preferred_element_type=jnp.float32)
            up_act = jnp.dot(rows_e, up_e[half], preferred_element_type=jnp.float32)
            act = (gate_act * jax.nn.sigmoid(ALPHA * gate_act) * (up_act + 1.0)).astype(jnp.bfloat16)
            part = jnp.dot(act, down_e[half], preferred_element_type=jnp.float32)
            summed = summed + lax.optimization_barrier(part.astype(jnp.bfloat16)).astype(jnp.float32)
        return lax.optimization_barrier(summed.astype(jnp.bfloat16))
    expert_out = lax.map(expert_forward, (slot_rows, w_gate, w_up, w_down))
    picked_out = from_slots(expert_out).astype(jnp.float32)
    mixed = lax.optimization_barrier(jnp.sum(gate_weights.reshape(blocks, TOK_DEV, TOPK, 1) * picked_out, axis=2)).reshape(SEQ, D)
    layer_out = (resid_f + mixed).astype(jnp.bfloat16)
    grad_f = out_grad.astype(jnp.float32)
    scaled = (gate_weights[:, :, None] * grad_f[:, None, :]).astype(jnp.bfloat16)
    grad_slots = to_slots(scaled.reshape(blocks, TOK_DEV, TOPK, D))

    def expert_backward(item):
        rows_e, grads_e, gate_e, up_e, down_e = item
        summed = jnp.zeros((rows_e.shape[0], D), jnp.float32)
        for half in range(2):
            gate_act = jnp.dot(rows_e, gate_e[half], preferred_element_type=jnp.float32)
            up_act = jnp.dot(rows_e, up_e[half], preferred_element_type=jnp.float32)
            sig = jax.nn.sigmoid(ALPHA * gate_act)
            act_grad = jnp.dot(grads_e, down_e[half].T, preferred_element_type=jnp.float32)
            gate_grad = (act_grad * (up_act + 1.0) * sig * (1.0 + ALPHA * gate_act * (1.0 - sig))).astype(jnp.bfloat16)
            up_grad = (act_grad * gate_act * sig).astype(jnp.bfloat16)
            part = jnp.dot(gate_grad, gate_e[half].T, preferred_element_type=jnp.float32) + jnp.dot(up_grad, up_e[half].T, preferred_element_type=jnp.float32)
            summed = summed + lax.optimization_barrier(part.astype(jnp.bfloat16)).astype(jnp.float32)
        return lax.optimization_barrier(summed.astype(jnp.bfloat16))
    normed_slots = lax.map(expert_backward, (slot_rows, grad_slots, w_gate, w_up, w_down))
    normed_grad = lax.optimization_barrier(jnp.sum(from_slots(normed_slots).astype(jnp.float32), axis=2)).reshape(SEQ, D)
    scaled_grad = norm_gain * normed_grad
    inner = lax.optimization_barrier(jnp.mean(resid_f * scaled_grad, axis=1, keepdims=True))
    resid_grad = (grad_f + inv_rms * scaled_grad - resid_f * (inv_rms * inv_rms * inv_rms) * inner).astype(jnp.bfloat16)
    attn_grad = lax.optimization_barrier(jnp.dot(resid_grad, out_weight.T, preferred_element_type=jnp.float32).astype(jnp.bfloat16))
    grad_heads = attn_grad.reshape(SEQ, HQ, DH).transpose(1, 0, 2)

    def head_backward(item):
        q_head, g_head, o_head, peak, total, head = item
        k_head = lax.dynamic_index_in_dim(keys, head // group, 0, keepdims=False)
        v_head = lax.dynamic_index_in_dim(values, head // group, 0, keepdims=False)

        def span_backward(carry, start):
            key_acc, value_acc = carry
            q_rows = lax.dynamic_slice_in_dim(q_head, start, stride, 0)
            g_rows = lax.dynamic_slice_in_dim(g_head, start, stride, 0)
            o_rows = lax.dynamic_slice_in_dim(o_head, start, stride, 0)
            peak_rows = lax.dynamic_slice_in_dim(peak, start, stride, 0)
            total_rows = lax.dynamic_slice_in_dim(total, start, stride, 0)
            key_span = lax.dynamic_slice_in_dim(k_head, start, stride + WINDOW, 0)
            value_rows = lax.dynamic_slice_in_dim(v_head, start, stride + WINDOW, 0)
            s = scores_of(q_rows, key_span, start)
            prob = jnp.exp(s - peak_rows[:, None]) / total_rows[:, None]
            delta = lax.optimization_barrier(jnp.sum(g_rows.astype(jnp.float32) * o_rows, axis=1))
            prob_grad = jnp.dot(g_rows, value_rows.T, preferred_element_type=jnp.float32)
            score_grad = (prob * (prob_grad - delta[:, None])).astype(jnp.bfloat16)
            q_grad = jnp.dot(score_grad, key_span, preferred_element_type=jnp.float32) * scale
            k_grad = jnp.dot(score_grad.T, q_rows, preferred_element_type=jnp.float32) * scale
            v_grad = jnp.dot(prob.astype(jnp.bfloat16).T, g_rows, preferred_element_type=jnp.float32)
            key_acc = lax.dynamic_update_slice_in_dim(key_acc, lax.dynamic_slice_in_dim(key_acc, start, stride + WINDOW, 0) + k_grad, start, 0)
            value_acc = lax.dynamic_update_slice_in_dim(value_acc, lax.dynamic_slice_in_dim(value_acc, start, stride + WINDOW, 0) + v_grad, start, 0)
            return ((key_acc, value_acc), q_grad)
        empty = jnp.zeros((SEQ + WINDOW, DH), jnp.float32)
        (key_acc, value_acc), q_grads = lax.scan(span_backward, (empty, empty), starts)
        return (q_grads.reshape(SEQ, DH), key_acc[WINDOW:], value_acc[WINDOW:])
    q_grads, k_grads, v_grads = lax.map(head_backward, (queries, grad_heads, outs, peaks, totals, heads))
    query_grad = q_grads.transpose(1, 0, 2).reshape(SEQ, HQ * DH).astype(jnp.bfloat16)
    key_grad = lax.optimization_barrier(jnp.sum(k_grads.reshape(KVH, group, SEQ, DH), axis=1)).transpose(1, 0, 2).reshape(SEQ, KVH * DH).astype(jnp.bfloat16)
    value_grad = lax.optimization_barrier(jnp.sum(v_grads.reshape(KVH, group, SEQ, DH), axis=1)).transpose(1, 0, 2).reshape(SEQ, KVH * DH).astype(jnp.bfloat16)
    return (layer_out, resid_grad, query_grad, key_grad, value_grad)
```

```python
import jax
import jax.numpy as jnp
from jax import lax
from jax.sharding import PartitionSpec as P

D = 2880
HQ = 32
KVH = 4
DH = 64
TOPK = 4
WINDOW = 128


NEG = -1e30
EPS = 1e-05
ALPHA = 1.702


def from_behind(value, axis, steps):
    count = lax.axis_size(axis)
    initial, last = (max(0, -steps), min(count, count - steps))
    return lax.ppermute(value, axis, [(source, source + steps) for source in range(initial, last)])


def band_mask(first, count):
    query_pos = first + jnp.arange(count, dtype=jnp.int32)
    key_pos = first - WINDOW + jnp.arange(count + WINDOW, dtype=jnp.int32)
    diff = query_pos[:, None] - key_pos[None, :]
    return (diff >= 0) & (diff < WINDOW) & (key_pos[None, :] >= 0)


def slot_targets(expert_ids, experts, capacity):
    flat = expert_ids.reshape(-1)
    table = jnp.arange(experts, dtype=jnp.int32)
    hits = (flat[:, None] == table[None, :]).astype(jnp.int32)
    before = jnp.cumsum(hits, axis=0) - hits
    slot = jnp.sum(before * hits, axis=1)
    return (flat * capacity + slot).reshape(expert_ids.shape)


def place(z_lo, x, z_hi, y, core):
    return (z_lo * 4 + x) * 16 + z_hi * 8 + y * 2 + core


def moves(step):
    pairs = []
    for source in range(128):
        outer, inner = divmod(source, 16)
        z_lo, x = divmod(outer, 4)
        z_hi, rest = divmod(inner, 8)
        y, core = divmod(rest, 2)
        x2, y2, z2, core2 = step(x, y, z_hi * 2 + z_lo, core)
        pairs.append((source, place(z2 % 2, x2 % 4, z2 // 2, y2 % 4, core2)))
    return pairs


AXES = ("ctx", "exp")
TO_PEER = moves(lambda x, y, z, core: (x, y, z, 1 - core))
TO_HIGH_Y = moves(lambda x, y, z, core: (x, y + 1, z, core))
TO_LOW_Y = moves(lambda x, y, z, core: (x, y - 1, z, core))
ACROSS_Z = moves(lambda x, y, z, core: (x, y, 3 - z, core))
CORE_GROUPS = [list(range(0, 128, 2)), list(range(1, 128, 2))]


def send(value, pairs):
    return lax.ppermute(value, AXES, pairs)


def gather_rows(block):
    half, quarter = D // 2, D // 4
    across = send(block, ACROSS_Z)
    below = send(block, TO_HIGH_Y)
    above = send(block, TO_LOW_Y)
    below_across_a = send(below[:, :half], ACROSS_Z)
    above_across_b = send(above[:, half:], ACROSS_Z)
    far_a = send(below[:, :half], TO_HIGH_Y)
    far_b = send(above[:, half:], TO_LOW_Y)
    below_across_b = send(across[:, half:], TO_HIGH_Y)
    above_across_a = send(across[:, :half], TO_LOW_Y)
    far_across_a = send(far_a, ACROSS_Z)
    far_across_b = send(below_across_b[:, :quarter], TO_HIGH_Y)
    far_across_c = send(above_across_b[:, quarter:], TO_LOW_Y)
    return jnp.concatenate(
        [
            block,
            above,
            jnp.concatenate([far_a, far_b], axis=1),
            below,
            across,
            jnp.concatenate([above_across_a, above_across_b], axis=1),
            jnp.concatenate([far_across_a, far_across_b, far_across_c], axis=1),
            jnp.concatenate([below_across_a, below_across_b], axis=1),
        ],
        axis=0,
    )


def from_own(value, z_hi, y):
    value = jnp.where(z_hi == 1, value[:, ::-1], value)
    value = jnp.where(y % 2 == 1, jnp.roll(value, -1, axis=2), value)
    return jnp.where(y >= 2, jnp.roll(value, -2, axis=2), value)


def to_place(value, z_hi, y):
    value = jnp.where(z_hi == 1, value[:, ::-1], value)
    value = jnp.where(y % 2 == 1, jnp.roll(value, 1, axis=2), value)
    return jnp.where(y >= 2, jnp.roll(value, 2, axis=2), value)


def contract_rows(left, right):
    return lax.dot_general(
        left, right, (((0,), (0,)), ((), ())), preferred_element_type=jnp.float32
    )


def contract_cols(left, right):
    return lax.dot_general(
        left, right, (((1,), (1,)), ((), ())), preferred_element_type=jnp.float32
    )


def per_device(
    hidden_in,
    query_proj,
    key_proj,
    value_proj,
    sink_logits,
    out_weight,
    norm_gain,
    expert_ids,
    gate_weights,
    gate_proj,
    up_proj,
    down_proj,
    out_grad,
):
    ctx_size = lax.axis_size("ctx")
    exp_size = lax.axis_size("exp")
    exp_index = lax.axis_index("exp")
    device = lax.axis_index("ctx") * exp_size + exp_index
    tok_dev = hidden_in.shape[0]
    first_row = device * tok_dev
    group = HQ // KVH
    scale = DH ** (-0.5)
    stride = min(512, tok_dev)
    experts = ctx_size * exp_size // 2
    capacity = tok_dev * TOPK // experts
    kv_rows = jnp.concatenate([key_proj, value_proj], axis=1)
    earlier = from_behind(kv_rows, ("ctx", "exp"), 1)
    extended = jnp.concatenate([earlier, kv_rows], axis=0)
    z_hi, chip_y, core = exp_index // 8, (exp_index // 2) % 4, exp_index % 2
    projection = gather_rows(out_weight)
    queries = query_proj.reshape(tok_dev, HQ, DH)

    def operands(start, kv_head):
        q_rows = queries[start : start + stride, kv_head * group : (kv_head + 1) * group]
        key_span = extended[start : start + stride + WINDOW, kv_head * DH : (kv_head + 1) * DH]
        value_rows = extended[
            start : start + stride + WINDOW, (KVH + kv_head) * DH : (KVH + kv_head + 1) * DH
        ]
        return (q_rows, key_span, value_rows)

    def scores_of(q_rows, key_span, start):
        allowed = band_mask(first_row + start, stride)
        scores = (
            jnp.einsum("thd,jd->htj", q_rows, key_span, preferred_element_type=jnp.float32) * scale
        )
        return jnp.where(allowed[None], scores, NEG)

    start = 0
    head_outs = []
    span_stats = []
    for kv_head in range(KVH):
        q_rows, key_span, value_rows = operands(start, kv_head)
        scores = scores_of(q_rows, key_span, start)
        sinks = sink_logits[kv_head * group : (kv_head + 1) * group][:, None]
        peak = jnp.maximum(jnp.max(scores, axis=2), sinks)
        weights = jnp.exp(scores - peak[:, :, None])
        total = jnp.sum(weights, axis=2) + jnp.exp(sinks - peak)
        summed = jnp.einsum(
            "htj,jd->thd",
            weights.astype(jnp.bfloat16),
            value_rows,
            preferred_element_type=jnp.float32,
        )
        head_outs.append(summed / total.T[:, :, None])
        span_stats.append((peak, total))
    stats = [span_stats]
    out_rows = jnp.concatenate(head_outs, axis=1)
    attn = out_rows.reshape(tok_dev, HQ * DH).astype(jnp.bfloat16)
    by_place = attn.reshape(tok_dev, 2, 4, 2, 2 * DH)
    first, second = by_place[:, :, :, 0], by_place[:, :, :, 1]
    mine = jnp.where(core == 0, first, second)
    theirs = send(jnp.where(core == 0, second, first), TO_PEER)
    mine = from_own(mine, z_hi, chip_y).reshape(tok_dev, HQ * DH // 2)
    theirs = from_own(theirs, z_hi, chip_y).reshape(tok_dev, HQ * DH // 2)
    for_peer = jnp.dot(theirs, projection, preferred_element_type=jnp.float32)
    attn_out = jnp.dot(mine, projection, preferred_element_type=jnp.float32)
    attn_out = attn_out + send(for_peer, TO_PEER)
    resid = lax.optimization_barrier(
        (hidden_in.astype(jnp.float32) + attn_out).astype(jnp.bfloat16)
    )
    resid_f = resid.astype(jnp.float32)
    inv_rms = lax.rsqrt(jnp.mean(resid_f * resid_f, axis=1, keepdims=True) + EPS)
    normed = (resid_f * inv_rms * norm_gain).astype(jnp.bfloat16)
    targets = slot_targets(expert_ids, experts, capacity)
    slot_table = jnp.arange(experts * capacity, dtype=jnp.int32)
    picks = (targets[:, :, None] == slot_table[None, None, :]).astype(jnp.bfloat16)
    placed = jnp.sum(picks, axis=1)

    def exchange(slots):
        return lax.all_to_all(
            slots.reshape(experts, capacity, D),
            AXES,
            split_axis=0,
            concat_axis=0,
            tiled=True,
            axis_index_groups=CORE_GROUPS,
        ).reshape(experts * capacity, D)

    def add_halves(own, received):
        return (own.astype(jnp.float32) + received.astype(jnp.float32)).astype(jnp.bfloat16)

    w_gate = gate_proj[0]
    w_up = up_proj[0]
    w_down = down_proj[0]
    grad_f = out_grad.astype(jnp.float32)
    slot_weight = jnp.sum(gate_weights[:, :, None] * picks.astype(jnp.float32), axis=(0, 1))
    grad_slots = (slot_weight[:, None] * contract_rows(placed, out_grad)).astype(jnp.bfloat16)
    grads_own = exchange(grad_slots)
    grads_peer = send(grads_own, TO_PEER)
    act_grad_own = contract_cols(grads_own, w_down)
    act_grad_peer = contract_cols(grads_peer, w_down)

    slots_in = contract_rows(placed, normed).astype(jnp.bfloat16)
    rows_own = exchange(slots_in)
    rows_peer = send(rows_own, TO_PEER)

    def hidden_units(rows, act_grad):
        gate_act = jnp.dot(rows, w_gate, preferred_element_type=jnp.float32)
        up_act = jnp.dot(rows, w_up, preferred_element_type=jnp.float32)
        sig = jax.nn.sigmoid(ALPHA * gate_act)
        act = (gate_act * sig * (up_act + 1.0)).astype(jnp.bfloat16)
        gate_grad = (
            act_grad * (up_act + 1.0) * sig * (1.0 + ALPHA * gate_act * (1.0 - sig))
        ).astype(jnp.bfloat16)
        up_grad = (act_grad * gate_act * sig).astype(jnp.bfloat16)
        return act, gate_grad, up_grad

    def row_grad_of(gate_grad, up_grad):
        return (contract_cols(gate_grad, w_gate) + contract_cols(up_grad, w_up)).astype(jnp.bfloat16)

    def part_of(act):
        return jnp.dot(act, w_down, preferred_element_type=jnp.float32).astype(jnp.bfloat16)

    act_own, gate_grad_own, up_grad_own = hidden_units(rows_own, act_grad_own)
    act_peer, gate_grad_peer, up_grad_peer = hidden_units(rows_peer, act_grad_peer)
    row_grad_peer = send(lax.optimization_barrier(row_grad_of(gate_grad_peer, up_grad_peer)), TO_PEER)
    row_grad_own = lax.optimization_barrier(row_grad_of(gate_grad_own, up_grad_own))
    row_grad = add_halves(row_grad_own, row_grad_peer)
    row_grad, act_own, act_peer = lax.optimization_barrier((row_grad, act_own, act_peer))
    normed_slots = exchange(row_grad)
    part_peer = send(lax.optimization_barrier(part_of(act_peer)), TO_PEER)
    part_own = lax.optimization_barrier(part_of(act_own))
    expert_out = exchange(add_halves(part_own, part_peer))

    combine = jnp.sum(gate_weights[:, :, None] * picks.astype(jnp.float32), axis=1)
    combine_high = combine.astype(jnp.bfloat16)
    combine_low = (combine - combine_high.astype(jnp.float32)).astype(jnp.bfloat16)
    mixed = jnp.dot(combine_high, expert_out, preferred_element_type=jnp.float32) + jnp.dot(
        combine_low, expert_out, preferred_element_type=jnp.float32
    )
    layer_out = (resid_f + mixed).astype(jnp.bfloat16)
    normed_grad = jnp.dot(placed, normed_slots, preferred_element_type=jnp.float32)
    scaled_grad = norm_gain * normed_grad
    inner = jnp.mean(resid_f * scaled_grad, axis=1, keepdims=True)
    resid_grad = (
        grad_f + inv_rms * scaled_grad - resid_f * (inv_rms * inv_rms * inv_rms) * inner
    ).astype(jnp.bfloat16)
    peer_grad = send(resid_grad, TO_PEER)
    grad_theirs = contract_cols(peer_grad, projection).astype(jnp.bfloat16)
    grad_mine = contract_cols(resid_grad, projection).astype(jnp.bfloat16)
    grad_back = send(to_place(grad_theirs.reshape(tok_dev, 2, 4, 2 * DH), z_hi, chip_y), TO_PEER)
    grad_mine = to_place(grad_mine.reshape(tok_dev, 2, 4, 2 * DH), z_hi, chip_y)
    attn_grad = jnp.where(
        core == 0,
        jnp.stack([grad_mine, grad_back], axis=3),
        jnp.stack([grad_back, grad_mine], axis=3),
    )
    attn_grad = lax.optimization_barrier(attn_grad.reshape(tok_dev, HQ * DH))
    grads = attn_grad.reshape(tok_dev, HQ, DH)
    delta_all = jnp.sum(grads.astype(jnp.float32) * out_rows, axis=2)
    kv_grad = jnp.zeros((tok_dev + WINDOW, 2 * KVH * DH), jnp.float32)
    start = 0
    head_parts = []
    for kv_head in range(KVH):
        peak, total = stats[start // stride][kv_head]
        q_rows, key_span, value_rows = operands(start, kv_head)
        g_rows = grads[start : start + stride, kv_head * group : (kv_head + 1) * group]
        delta = delta_all[start : start + stride, kv_head * group : (kv_head + 1) * group].T
        scores = scores_of(q_rows, key_span, start)
        prob = jnp.exp(scores - peak[:, :, None]) / total[:, :, None]
        prob_grad = jnp.einsum(
            "thd,jd->htj", g_rows, value_rows, preferred_element_type=jnp.float32
        )
        score_grad = (prob * (prob_grad - delta[:, :, None])).astype(jnp.bfloat16)
        head_parts.append(
            jnp.einsum("htj,jd->thd", score_grad, key_span, preferred_element_type=jnp.float32)
            * scale
        )
        key_part = (
            jnp.einsum("htj,thd->jd", score_grad, q_rows, preferred_element_type=jnp.float32)
            * scale
        )
        value_part = jnp.einsum(
            "htj,thd->jd", prob.astype(jnp.bfloat16), g_rows, preferred_element_type=jnp.float32
        )
        kv_grad = kv_grad.at[
            start : start + stride + WINDOW, kv_head * DH : (kv_head + 1) * DH
        ].add(key_part)
        kv_grad = kv_grad.at[
            start : start + stride + WINDOW, (KVH + kv_head) * DH : (KVH + kv_head + 1) * DH
        ].add(value_part)
    query_rows = jnp.concatenate(head_parts, axis=1)
    returned = from_behind(kv_grad[:WINDOW].astype(jnp.bfloat16), ("ctx", "exp"), -1).astype(
        jnp.float32
    )
    own = kv_grad[WINDOW:]
    own = own.at[tok_dev - WINDOW :].add(returned)
    key_grad = own[:, : KVH * DH].astype(jnp.bfloat16)
    value_grad = own[:, KVH * DH :].astype(jnp.bfloat16)
    query_grad = query_rows.reshape(tok_dev, HQ * DH).astype(jnp.bfloat16)
    return (layer_out, resid_grad, query_grad, key_grad, value_grad)


def solution(mesh):
    in_specs = (
        P(("ctx", "exp"), None),
        P(("ctx", "exp"), None),
        P(("ctx", "exp"), None),
        P(("ctx", "exp"), None),
        P(),
        P("exp", None),
        P(),
        P(("ctx", "exp"), None),
        P(("ctx", "exp"), None),
        P(("ctx", "exp"), None, None),
        P(("ctx", "exp"), None, None),
        P(("ctx", "exp"), None, None),
        P(("ctx", "exp"), None),
    )
    out_specs = (
        P(("ctx", "exp"), None),
        P(("ctx", "exp"), None),
        P(("ctx", "exp"), None),
        P(("ctx", "exp"), None),
        P(("ctx", "exp"), None),
    )
    return jax.shard_map(
        per_device, mesh=mesh, in_specs=in_specs, out_specs=out_specs, check_vma=False
    )
```

```python
import jax
import jax.numpy as jnp
from jax import lax
from jax.experimental import pallas as pl
from jax.experimental.layout import Layout, with_layout_constraint
from jax.experimental.pallas import tpu as pltpu
from jax.sharding import PartitionSpec as P

D = 2880
HQ = 32
KVH = 4
DH = 64
TOPK = 4
WINDOW = 128


NEG = -1e30
EPS = 1e-05
ALPHA = 1.702


def from_behind(value, axis, steps):
    count = lax.axis_size(axis)
    initial, last = (max(0, -steps), min(count, count - steps))
    return lax.ppermute(value, axis, [(source, source + steps) for source in range(initial, last)])


def band_mask(first, count):
    query_pos = first + jnp.arange(count, dtype=jnp.int32)
    key_pos = first - WINDOW + jnp.arange(count + WINDOW, dtype=jnp.int32)
    diff = query_pos[:, None] - key_pos[None, :]
    return (diff >= 0) & (diff < WINDOW) & (key_pos[None, :] >= 0)


def slot_targets(expert_ids, experts, capacity):
    flat = expert_ids.reshape(-1)
    table = jnp.arange(experts, dtype=jnp.int32)
    hits = (flat[:, None] == table[None, :]).astype(jnp.int32)
    before = jnp.cumsum(hits, axis=0) - hits
    slot = jnp.sum(before * hits, axis=1)
    return (flat * capacity + slot).reshape(expert_ids.shape)


def place(z_lo, x, z_hi, y, core):
    return (z_lo * 4 + x) * 16 + z_hi * 8 + y * 2 + core


def moves(step):
    pairs = []
    for source in range(128):
        outer, inner = divmod(source, 16)
        z_lo, x = divmod(outer, 4)
        z_hi, rest = divmod(inner, 8)
        y, core = divmod(rest, 2)
        x2, y2, z2, core2 = step(x, y, z_hi * 2 + z_lo, core)
        pairs.append((source, place(z2 % 2, x2 % 4, z2 // 2, y2 % 4, core2)))
    return pairs


AXES = ("ctx", "exp")
TO_PEER = moves(lambda x, y, z, core: (x, y, z, 1 - core))
TO_HIGH_Y = moves(lambda x, y, z, core: (x, y + 1, z, core))
TO_LOW_Y = moves(lambda x, y, z, core: (x, y - 1, z, core))
ACROSS_Z = moves(lambda x, y, z, core: (x, y, 3 - z, core))
HIGH_Y_ACROSS = moves(lambda x, y, z, core: (x, y + 1, 3 - z, core))
LOW_Y_ACROSS = moves(lambda x, y, z, core: (x, y - 1, 3 - z, core))
CORE_GROUPS = [list(range(0, 128, 2)), list(range(1, 128, 2))]


def send(value, pairs):
    return lax.ppermute(value, AXES, pairs)


def by_rows(value):
    return with_layout_constraint(value, Layout(tuple(range(value.ndim))))


def by_columns(value):
    return with_layout_constraint(value, Layout((1, 0)))


def near_blocks(block):
    return send(block, TO_LOW_Y), send(block, TO_HIGH_Y), send(block, ACROSS_Z)


def far_blocks(above, below, across):
    third, half = D // 3, D // 2
    up = send(jnp.concatenate([across[:, third:], below[:, :half]], axis=1), TO_HIGH_Y)
    down = send(jnp.concatenate([across[:, : 2 * third], above[:, half:]], axis=1), TO_LOW_Y)
    over = send(jnp.concatenate([below[:, :third], above[:, 2 * third :]], axis=1), ACROSS_Z)
    up_over = send(below[:, :half], HIGH_Y_ACROSS)
    down_over = send(above[:, half:], LOW_Y_ACROSS)
    return up, down, over, up_over, down_over


THIRD, HALF_D = D // 3, D // 2
SOURCES = {
    0: [(0, D, 0, 0)],
    1: [(0, D, 1, 0)],
    3: [(0, D, 2, 0)],
    4: [(0, D, 3, 0)],
    7: [(0, THIRD, 6, 0), (THIRD, 2 * THIRD, 4, 0)],
    2: [(0, HALF_D, 4, 2 * THIRD), (HALF_D, HALF_D, 5, 2 * THIRD)],
    5: [(0, 2 * THIRD, 5, 0), (2 * THIRD, THIRD, 6, THIRD)],
    6: [(0, HALF_D, 7, 0), (HALF_D, HALF_D, 8, 0)],
}


def place_of(where, place):
    z_hi = (where[0] + place // 4) % 2
    return z_hi * 4 + (where[1] + place % 4) % 4


def collect_body(where, *refs):
    *parts, columns, joined, product = refs
    rows = parts[0].shape[1]
    picked = jnp.concatenate(
        [columns[pl.ds(place_of(where, place) * rows, rows), :] for place in range(8)], axis=0
    )
    edges = (0, THIRD, HALF_D, 2 * THIRD, D)
    for first, last in zip(edges[:-1], edges[1:]):
        found = []
        for place in range(8):
            for start, count, index, offset in SOURCES[place]:
                if start <= first and last <= start + count:
                    at = offset + first - start
                    found.append(parts[index][at : at + last - first, :])
        side = jnp.concatenate(found, axis=1)
        joined[first:last, :] = side
        product[first:last, :] = jnp.dot(side, picked, preferred_element_type=jnp.float32)


def collect(where, parts, columns):
    return in_vmem(
        collect_body,
        [
            jax.ShapeDtypeStruct((D, columns.shape[0]), jnp.bfloat16),
            jax.ShapeDtypeStruct((D, columns.shape[1]), jnp.float32),
        ],
        *[part.T for part in parts],
        columns,
        scalars=where,
        mib=24,
    )


def contract_rows(left, right):
    return lax.dot_general(
        left, right, (((0,), (0,)), ((), ())), preferred_element_type=jnp.float32
    )


def contract_cols(left, right):
    return lax.dot_general(
        left, right, (((1,), (1,)), ((), ())), preferred_element_type=jnp.float32
    )


def in_vmem(body, out_shape, *operands, scalars=None, mib=16):
    spec = pl.BlockSpec(memory_space=pltpu.VMEM)
    in_specs = [spec] * len(operands)
    if scalars is not None:
        in_specs = [pl.BlockSpec(memory_space=pltpu.SMEM)] + in_specs
        operands = (scalars, *operands)
    return pl.pallas_call(
        body,
        out_shape=out_shape,
        in_specs=in_specs,
        out_specs=jax.tree.map(lambda _: spec, out_shape),
        compiler_params=pltpu.CompilerParams(vmem_limit_bytes=mib * 1024 * 1024),
        cost_estimate=pl.CostEstimate(flops=1000, bytes_accessed=1000, transcendentals=0),
    )(*operands)


def resid_grad_body(placed, slots, resid, grad, inv_rms, gain, out):
    normed_grad = jnp.dot(placed[...], slots[...], preferred_element_type=jnp.float32)
    scaled = gain[...] * normed_grad
    resid_f = resid[...].astype(jnp.float32)
    inv = inv_rms[...]
    inner = jnp.sum(resid_f * scaled, axis=1, keepdims=True) * (1.0 / D)
    value = grad[...].astype(jnp.float32) + inv * scaled - resid_f * (inv * inv * inv) * inner
    out[...] = value.astype(jnp.bfloat16)


def attn_grad_body(where, resid_grad, projection, out):
    rows = resid_grad.shape[0]
    grad = jnp.dot(resid_grad[...], projection[...], preferred_element_type=jnp.float32).T
    for place in range(8):
        out[pl.ds(place_of(where, place) * rows, rows), :] = grad[
            place * rows : (place + 1) * rows
        ].astype(jnp.bfloat16)


def down_body(act, weight, out):
    out[...] = contract_rows(act[...], weight[...]).astype(jnp.bfloat16)


def down_add_body(act, weight, received, out):
    rows = 128
    for start in range(0, act.shape[1], rows):
        at = pl.ds(start, rows)
        own = contract_rows(act[:, at], weight[...])
        own = own.astype(jnp.bfloat16).astype(jnp.float32)
        out[at, :] = (own + received[at, :].astype(jnp.float32)).astype(jnp.bfloat16)


def mix_body(high, low, expert_out, resid, out):
    mixed = jnp.dot(high[...], expert_out[...], preferred_element_type=jnp.float32)
    mixed = mixed + jnp.dot(low[...], expert_out[...], preferred_element_type=jnp.float32)
    value = resid[...].astype(jnp.float32) + mixed
    for start in range(0, D, 128):
        last = min(D, start + 128)
        out[start:last, :] = value[:, start:last].T.astype(jnp.bfloat16)


def per_device(
    hidden_in,
    query_proj,
    key_proj,
    value_proj,
    sink_logits,
    out_weight,
    norm_gain,
    expert_ids,
    gate_weights,
    gate_proj,
    up_proj,
    down_proj,
    out_grad,
):
    ctx_size = lax.axis_size("ctx")
    exp_size = lax.axis_size("exp")
    exp_index = lax.axis_index("exp")
    device = lax.axis_index("ctx") * exp_size + exp_index
    tok_dev = hidden_in.shape[0]
    first_row = device * tok_dev
    group = HQ // KVH
    scale = DH ** (-0.5)
    stride = min(512, tok_dev)
    experts = ctx_size * exp_size // 2
    capacity = tok_dev * TOPK // experts
    above, below, across = near_blocks(out_weight)
    kv_rows = jnp.concatenate([key_proj, value_proj], axis=1)
    earlier = from_behind(kv_rows, ("ctx", "exp"), 1)
    above, below, across, earlier = lax.optimization_barrier((above, below, across, earlier))
    far = far_blocks(above, below, across)
    where = jnp.stack([exp_index // 8, (exp_index // 2) % 4]).astype(jnp.int32)
    extended = jnp.concatenate([earlier, kv_rows], axis=0)
    core = exp_index % 2
    queries = query_proj.reshape(tok_dev, HQ, DH)

    def operands(start, kv_head):
        q_rows = queries[start : start + stride, kv_head * group : (kv_head + 1) * group]
        key_span = extended[start : start + stride + WINDOW, kv_head * DH : (kv_head + 1) * DH]
        value_rows = extended[
            start : start + stride + WINDOW, (KVH + kv_head) * DH : (KVH + kv_head + 1) * DH
        ]
        return (q_rows, key_span, value_rows)

    def scores_of(q_rows, key_span, start):
        allowed = band_mask(first_row + start, stride)
        scores = (
            jnp.einsum("thd,jd->htj", q_rows, key_span, preferred_element_type=jnp.float32) * scale
        )
        return jnp.where(allowed[None], scores, NEG)

    start = 0
    head_outs = []
    span_stats = []
    for kv_head in range(KVH):
        q_rows, key_span, value_rows = operands(start, kv_head)
        scores = scores_of(q_rows, key_span, start)
        sinks = sink_logits[kv_head * group : (kv_head + 1) * group][:, None]
        peak = jnp.maximum(jnp.max(scores, axis=2), sinks)
        weights = jnp.exp(scores - peak[:, :, None])
        total = jnp.sum(weights, axis=2) + jnp.exp(sinks - peak)
        summed = jnp.einsum(
            "htj,jd->thd",
            weights.astype(jnp.bfloat16),
            value_rows,
            preferred_element_type=jnp.float32,
        )
        head_outs.append(summed / total.T[:, :, None])
        span_stats.append((peak, total))
    stats = [span_stats]
    out_rows = jnp.concatenate(head_outs, axis=1)
    attn = out_rows.reshape(tok_dev, HQ * DH).astype(jnp.bfloat16)
    by_place = attn.reshape(tok_dev, 8, 2, 2 * DH)
    first, second = by_place[:, :, 0], by_place[:, :, 1]
    theirs = send(jnp.where(core == 0, second, first), TO_PEER).reshape(tok_dev, HQ * DH // 2)
    mine = jnp.where(core == 0, first, second).reshape(tok_dev, HQ * DH // 2)
    targets = slot_targets(expert_ids, experts, capacity)
    slot_table = jnp.arange(experts * capacity, dtype=jnp.int32)
    picks = (targets[:, :, None] == slot_table[None, None, :]).astype(jnp.bfloat16)
    placed = jnp.sum(picks, axis=1)
    grad_f = out_grad.astype(jnp.float32)
    slot_weight = jnp.sum(gate_weights[:, :, None] * picks.astype(jnp.float32), axis=(0, 1))
    grad_slots = (slot_weight[:, None] * contract_rows(placed, out_grad)).astype(jnp.bfloat16)
    grad_slots = by_rows(grad_slots)
    up, down, over, up_over, down_over = far
    grad_slots, up_over, down_over = lax.optimization_barrier((grad_slots, up_over, down_over))
    joined, both = collect(
        where,
        (out_weight, above, below, across, up, down, over, up_over, down_over),
        jnp.concatenate([mine.T, theirs.T], axis=1),
    )
    attn_out = both[:, :tok_dev].T + send(both[:, tok_dev:].T, TO_PEER)
    resid = lax.optimization_barrier(
        (hidden_in.astype(jnp.float32) + attn_out).astype(jnp.bfloat16)
    )
    resid = by_columns(resid)
    resid_f = resid.astype(jnp.float32)
    inv_rms = lax.rsqrt(jnp.mean(resid_f * resid_f, axis=1, keepdims=True) + EPS)
    normed = (resid_f * inv_rms * norm_gain).astype(jnp.bfloat16)
    def exchange(slots):
        return lax.all_to_all(
            slots.reshape(experts, capacity, D),
            AXES,
            split_axis=0,
            concat_axis=0,
            tiled=True,
            axis_index_groups=CORE_GROUPS,
        )

    def swap(value):
        return send(by_rows(value.reshape(experts, capacity, D)), TO_PEER)

    def flat(value):
        return by_rows(by_rows(value).reshape(experts * capacity, D))

    def add_halves(own, received):
        return (own.astype(jnp.float32) + received.astype(jnp.float32)).astype(jnp.bfloat16)

    w_gate = gate_proj[0]
    w_up = up_proj[0]
    w_down = down_proj[0]
    grads_own = exchange(grad_slots)
    grads_peer = flat(swap(grads_own))
    act_grad_own = by_columns(contract_cols(flat(grads_own), w_down))
    act_grad_peer = by_columns(contract_cols(grads_peer, w_down))

    slots_in = contract_rows(placed, normed).astype(jnp.bfloat16)
    rows_own, act_grad_own, act_grad_peer, resid_rows, grad_rows = lax.optimization_barrier(
        (exchange(by_rows(slots_in)), act_grad_own, act_grad_peer, by_rows(resid), by_rows(out_grad))
    )
    rows_peer = flat(swap(rows_own))
    rows_own = flat(rows_own)

    def hidden_units(rows, act_grad):
        gate_act = jnp.dot(rows, w_gate, preferred_element_type=jnp.float32)
        up_act = jnp.dot(rows, w_up, preferred_element_type=jnp.float32)
        sig = jax.nn.sigmoid(ALPHA * gate_act)
        act = (gate_act * sig * (up_act + 1.0)).astype(jnp.bfloat16)
        gate_grad = (
            act_grad * (up_act + 1.0) * sig * (1.0 + ALPHA * gate_act * (1.0 - sig))
        ).astype(jnp.bfloat16)
        up_grad = (act_grad * gate_act * sig).astype(jnp.bfloat16)
        return act, gate_grad, up_grad

    def row_grad_of(gate_grad, up_grad):
        return (contract_cols(gate_grad, w_gate) + contract_cols(up_grad, w_up)).astype(jnp.bfloat16)

    act_own, gate_grad_own, up_grad_own = hidden_units(rows_own, act_grad_own)
    rows_peer, act_own, gate_grad_own, up_grad_own = lax.optimization_barrier(
        (rows_peer, act_own, gate_grad_own, up_grad_own)
    )
    act_peer, gate_grad_peer, up_grad_peer = hidden_units(rows_peer, act_grad_peer)
    row_grad_peer = flat(swap(by_rows(row_grad_of(gate_grad_peer, up_grad_peer))))
    row_grad_own = lax.optimization_barrier(by_rows(row_grad_of(gate_grad_own, up_grad_own)))
    row_grad = by_rows(add_halves(row_grad_own, row_grad_peer))
    row_grad, act_own, act_peer = lax.optimization_barrier((row_grad, act_own, act_peer))
    normed_slots = flat(exchange(row_grad))
    rows_shape = jax.ShapeDtypeStruct((experts * capacity, D), jnp.bfloat16)
    part_peer = flat(swap(in_vmem(down_body, rows_shape, by_columns(act_peer).T, w_down)))
    part_sum = in_vmem(down_add_body, rows_shape, by_columns(act_own).T, w_down, part_peer)
    normed_slots, part_sum = lax.optimization_barrier((normed_slots, part_sum))
    expert_out = flat(exchange(part_sum))

    combine = jnp.sum(gate_weights[:, :, None] * picks.astype(jnp.float32), axis=1)
    combine_high = combine.astype(jnp.bfloat16)
    combine_low = (combine - combine_high.astype(jnp.float32)).astype(jnp.bfloat16)
    layer_out = in_vmem(
        mix_body,
        jax.ShapeDtypeStruct((D, tok_dev), jnp.bfloat16),
        combine_high,
        combine_low,
        expert_out,
        resid_rows,
    ).T
    resid_grad = in_vmem(
        resid_grad_body,
        jax.ShapeDtypeStruct((tok_dev, D), jnp.bfloat16),
        placed,
        normed_slots,
        resid_rows,
        grad_rows,
        inv_rms,
        norm_gain.reshape(1, D),
    )
    peer_grad = send(resid_grad.reshape(tok_dev // 8, 8, D), TO_PEER).reshape(tok_dev, D)

    def attn_grad_of(value):
        return in_vmem(
            attn_grad_body,
            jax.ShapeDtypeStruct((HQ * DH // 2, tok_dev), jnp.bfloat16),
            value,
            joined,
            scalars=where,
        ).reshape(8, 2 * DH, tok_dev)

    grad_mine = attn_grad_of(resid_grad)
    grad_back = send(attn_grad_of(peer_grad), TO_PEER)
    attn_grad = jnp.where(
        core == 0,
        jnp.stack([grad_mine, grad_back], axis=1),
        jnp.stack([grad_back, grad_mine], axis=1),
    )
    attn_grad = lax.optimization_barrier(attn_grad.reshape(HQ * DH, tok_dev).T)
    grads = attn_grad.reshape(tok_dev, HQ, DH)
    delta_all = jnp.sum(grads.astype(jnp.float32) * out_rows, axis=2)
    key_parts, value_parts = [], []
    start = 0
    head_parts = []
    for kv_head in range(KVH):
        peak, total = stats[start // stride][kv_head]
        q_rows, key_span, value_rows = operands(start, kv_head)
        g_rows = grads[start : start + stride, kv_head * group : (kv_head + 1) * group]
        delta = delta_all[start : start + stride, kv_head * group : (kv_head + 1) * group].T
        scores = scores_of(q_rows, key_span, start)
        prob = jnp.exp(scores - peak[:, :, None]) / total[:, :, None]
        prob_grad = jnp.einsum(
            "thd,jd->htj", g_rows, value_rows, preferred_element_type=jnp.float32
        )
        score_grad = (prob * (prob_grad - delta[:, :, None])).astype(jnp.bfloat16)
        head_parts.append(
            jnp.einsum("htj,jd->thd", score_grad, key_span, preferred_element_type=jnp.float32)
            * scale
        )
        key_part = (
            jnp.einsum("htj,thd->jd", score_grad, q_rows, preferred_element_type=jnp.float32)
            * scale
        )
        value_part = jnp.einsum(
            "htj,thd->jd", prob.astype(jnp.bfloat16), g_rows, preferred_element_type=jnp.float32
        )
        key_parts.append(key_part)
        value_parts.append(value_part)
    kv_grad = jnp.concatenate(key_parts + value_parts, axis=1)
    query_rows = jnp.concatenate(head_parts, axis=1)
    returned = from_behind(kv_grad[:WINDOW].astype(jnp.bfloat16), ("ctx", "exp"), -1).astype(
        jnp.float32
    )
    own = kv_grad[WINDOW:]
    own = own.at[tok_dev - WINDOW :].add(returned)
    key_grad = own[:, : KVH * DH].astype(jnp.bfloat16)
    value_grad = own[:, KVH * DH :].astype(jnp.bfloat16)
    query_grad = query_rows.reshape(tok_dev, HQ * DH).astype(jnp.bfloat16)
    return (layer_out, resid_grad, query_grad, key_grad, value_grad)


def solution(mesh):
    in_specs = (
        P(("ctx", "exp"), None),
        P(("ctx", "exp"), None),
        P(("ctx", "exp"), None),
        P(("ctx", "exp"), None),
        P(),
        P("exp", None),
        P(),
        P(("ctx", "exp"), None),
        P(("ctx", "exp"), None),
        P(("ctx", "exp"), None, None),
        P(("ctx", "exp"), None, None),
        P(("ctx", "exp"), None, None),
        P(("ctx", "exp"), None),
    )
    out_specs = (
        P(("ctx", "exp"), None),
        P(("ctx", "exp"), None),
        P(("ctx", "exp"), None),
        P(("ctx", "exp"), None),
        P(("ctx", "exp"), None),
    )
    return jax.shard_map(
        per_device, mesh=mesh, in_specs=in_specs, out_specs=out_specs, check_vma=False
    )
```

```python
import jax
import jax.numpy as jnp
from jax import lax
from jax.experimental import pallas as pl
from jax.experimental.layout import Layout, with_layout_constraint
from jax.experimental.pallas import tpu as pltpu
from jax.sharding import PartitionSpec as P

D = 2880
HQ = 32
KVH = 4
DH = 64
TOPK = 4
WINDOW = 128


NEG = -1e30
EPS = 1e-05
ALPHA = 1.702


def from_behind(value, axis, steps):
    count = lax.axis_size(axis)
    initial, last = (max(0, -steps), min(count, count - steps))
    return lax.ppermute(value, axis, [(source, source + steps) for source in range(initial, last)])


def band_mask(first, count):
    query_pos = first + jnp.arange(count, dtype=jnp.int32)
    key_pos = first - WINDOW + jnp.arange(count + WINDOW, dtype=jnp.int32)
    diff = query_pos[:, None] - key_pos[None, :]
    return (diff >= 0) & (diff < WINDOW) & (key_pos[None, :] >= 0)


def slot_targets(expert_ids, experts, capacity):
    flat = expert_ids.reshape(-1)
    table = jnp.arange(experts, dtype=jnp.int32)
    hits = (flat[:, None] == table[None, :]).astype(jnp.int32)
    before = jnp.cumsum(hits, axis=0) - hits
    slot = jnp.sum(before * hits, axis=1)
    return (flat * capacity + slot).reshape(expert_ids.shape)


def place(z_lo, x, z_hi, y, core):
    return (z_lo * 4 + x) * 16 + z_hi * 8 + y * 2 + core


def moves(step):
    pairs = []
    for source in range(128):
        outer, inner = divmod(source, 16)
        z_lo, x = divmod(outer, 4)
        z_hi, rest = divmod(inner, 8)
        y, core = divmod(rest, 2)
        x2, y2, z2, core2 = step(x, y, z_hi * 2 + z_lo, core)
        pairs.append((source, place(z2 % 2, x2 % 4, z2 // 2, y2 % 4, core2)))
    return pairs


AXES = ("ctx", "exp")
TO_PEER = moves(lambda x, y, z, core: (x, y, z, 1 - core))
TO_HIGH_Y = moves(lambda x, y, z, core: (x, y + 1, z, core))
TO_LOW_Y = moves(lambda x, y, z, core: (x, y - 1, z, core))
ACROSS_Z = moves(lambda x, y, z, core: (x, y, 3 - z, core))
HIGH_Y_ACROSS = moves(lambda x, y, z, core: (x, y + 1, 3 - z, core))
LOW_Y_ACROSS = moves(lambda x, y, z, core: (x, y - 1, 3 - z, core))
CORE_GROUPS = [list(range(0, 128, 2)), list(range(1, 128, 2))]


def send(value, pairs):
    return lax.ppermute(value, AXES, pairs)


def by_rows(value):
    return with_layout_constraint(value, Layout(tuple(range(value.ndim))))


def by_columns(value):
    return with_layout_constraint(value, Layout((1, 0)))


def near_blocks(block):
    return send(block, TO_LOW_Y), send(block, TO_HIGH_Y), send(block, ACROSS_Z)


def far_blocks(above, below, across):
    third, half = D // 3, D // 2
    up = send(jnp.concatenate([across[:, third:], below[:, :half]], axis=1), TO_HIGH_Y)
    down = send(jnp.concatenate([across[:, : 2 * third], above[:, half:]], axis=1), TO_LOW_Y)
    over = send(jnp.concatenate([below[:, :third], above[:, 2 * third :]], axis=1), ACROSS_Z)
    up_over = send(below[:, :half], HIGH_Y_ACROSS)
    down_over = send(above[:, half:], LOW_Y_ACROSS)
    return up, down, over, up_over, down_over


THIRD, HALF_D = D // 3, D // 2
SOURCES = {
    0: [(0, D, 0, 0)],
    1: [(0, D, 1, 0)],
    3: [(0, D, 2, 0)],
    4: [(0, D, 3, 0)],
    7: [(0, THIRD, 6, 0), (THIRD, 2 * THIRD, 4, 0)],
    2: [(0, HALF_D, 4, 2 * THIRD), (HALF_D, HALF_D, 5, 2 * THIRD)],
    5: [(0, 2 * THIRD, 5, 0), (2 * THIRD, THIRD, 6, THIRD)],
    6: [(0, HALF_D, 7, 0), (HALF_D, HALF_D, 8, 0)],
}


def place_of(where, place):
    z_hi = (where[0] + place // 4) % 2
    return z_hi * 4 + (where[1] + place % 4) % 4


def collect_body(where, *refs):
    *parts, columns, joined, for_peer, for_own = refs
    rows = parts[0].shape[1]
    picked = jnp.concatenate(
        [columns[pl.ds(place_of(where, place) * rows, rows), :] for place in range(8)], axis=0
    )
    edges = (0, THIRD, HALF_D, 2 * THIRD, D)
    for first, last in zip(edges[:-1], edges[1:]):
        found = []
        for place in range(8):
            for start, count, index, offset in SOURCES[place]:
                if start <= first and last <= start + count:
                    at = offset + first - start
                    found.append(parts[index][at : at + last - first, :])
        side = jnp.concatenate(found, axis=1)
        joined[first:last, :] = side
        product = jnp.dot(side, picked, preferred_element_type=jnp.float32)
        for_peer[first:last, :] = product[:, :rows]
        for_own[first:last, :] = product[:, rows:]


def collect(where, parts, columns):
    product = jax.ShapeDtypeStruct((D, columns.shape[1] // 2), jnp.float32)
    return in_vmem(
        collect_body,
        [jax.ShapeDtypeStruct((D, columns.shape[0]), jnp.bfloat16), product, product],
        *[part.T for part in parts],
        columns,
        scalars=where,
        mib=24,
    )


def contract_rows(left, right):
    return lax.dot_general(
        left, right, (((0,), (0,)), ((), ())), preferred_element_type=jnp.float32
    )


def contract_cols(left, right):
    return lax.dot_general(
        left, right, (((1,), (1,)), ((), ())), preferred_element_type=jnp.float32
    )


def in_vmem(body, out_shape, *operands, scalars=None, mib=16):
    spec = pl.BlockSpec(memory_space=pltpu.VMEM)
    in_specs = [spec] * len(operands)
    if scalars is not None:
        in_specs = [pl.BlockSpec(memory_space=pltpu.SMEM)] + in_specs
        operands = (scalars, *operands)
    return pl.pallas_call(
        body,
        out_shape=out_shape,
        in_specs=in_specs,
        out_specs=jax.tree.map(lambda _: spec, out_shape),
        compiler_params=pltpu.CompilerParams(vmem_limit_bytes=mib * 1024 * 1024),
        cost_estimate=pl.CostEstimate(flops=1000, bytes_accessed=1000, transcendentals=0),
    )(*operands)


def resid_grad_body(placed, slots, resid, grad, inv_rms, gain, out):
    normed_grad = jnp.dot(placed[...], slots[...], preferred_element_type=jnp.float32)
    scaled = gain[...] * normed_grad
    resid_f = resid[...].astype(jnp.float32)
    inv = inv_rms[...]
    inner = jnp.sum(resid_f * scaled, axis=1, keepdims=True) * (1.0 / D)
    value = grad[...].astype(jnp.float32) + inv * scaled - resid_f * (inv * inv * inv) * inner
    out[...] = value.astype(jnp.bfloat16)


def attn_grad_body(where, resid_grad, projection, out):
    rows = resid_grad.shape[0]
    grad = jnp.dot(resid_grad[...], projection[...], preferred_element_type=jnp.float32).T
    for place in range(8):
        out[pl.ds(place_of(where, place) * rows, rows), :] = grad[
            place * rows : (place + 1) * rows
        ].astype(jnp.bfloat16)


def down_body(act, weight, out):
    out[...] = contract_rows(act[...], weight[...]).astype(jnp.bfloat16)


def down_add_body(act, weight, *refs):
    *quarters, out = refs
    rows = act.shape[1] // len(quarters)
    for number, received in enumerate(quarters):
        at = pl.ds(number * rows, rows)
        own = contract_rows(act[:, at], weight[...])
        own = own.astype(jnp.bfloat16).astype(jnp.float32)
        out[at, :] = (own + received[...].astype(jnp.float32)).astype(jnp.bfloat16)


def attn_back_body(first_block, sinks, queries, grads, keys, turned, values, dq, before, own):
    tokens = queries.shape[1]
    span = keys.shape[1]
    key_at = lax.broadcasted_iota(jnp.int32, (span, 2 * tokens), 0)
    lane = lax.broadcasted_iota(jnp.int32, (1, 2 * tokens), 1)
    token = lax.rem(lane, tokens)
    allowed = (key_at > token) & (key_at <= token + WINDOW)
    allowed = allowed & (key_at >= WINDOW * first_block[0])
    scale = DH ** (-0.5)
    group = HQ // KVH

    def two_heads(ref, head):
        return jnp.concatenate(
            [ref[head * DH : (head + 1) * DH, :], ref[(head + 1) * DH : (head + 2) * DH, :]], axis=1
        )

    key_grads, value_grads = [], []
    for kv_head in range(KVH):
        key_rows, value_rows, key_columns = keys[kv_head], values[kv_head], turned[kv_head]
        score_grads, probs, q_parts, g_parts = [], [], [], []
        for head in range(kv_head * group, (kv_head + 1) * group, 2):
            q, g = two_heads(queries, head), two_heads(grads, head)
            scores = jnp.dot(key_rows, q, preferred_element_type=jnp.float32) * scale
            scores = jnp.where(allowed, scores, NEG)
            sink = jnp.where(lane < tokens, sinks[head], sinks[head + 1])
            peak = jnp.maximum(jnp.max(scores, axis=0, keepdims=True), sink)
            weights = jnp.exp(scores - peak)
            total = jnp.sum(weights, axis=0, keepdims=True) + jnp.exp(sink - peak)
            inverse = 1.0 / total
            prob_grad = jnp.dot(value_rows, g, preferred_element_type=jnp.float32)
            rounded = weights.astype(jnp.bfloat16).astype(jnp.float32)
            delta = jnp.sum(rounded * prob_grad, axis=0, keepdims=True) * inverse
            prob = weights * inverse
            score_grad = (prob * (prob_grad - delta)).astype(jnp.bfloat16)
            turned_dq = jnp.dot(key_columns, score_grad, preferred_element_type=jnp.float32) * scale
            both = jnp.concatenate([turned_dq[:, :tokens], turned_dq[:, tokens:]], axis=0)
            dq[:, head * DH : (head + 2) * DH] = both.T.astype(jnp.bfloat16)
            score_grads.append(score_grad)
            probs.append(prob.astype(jnp.bfloat16))
            q_parts.append(q)
            g_parts.append(g)
        key_grads.append(
            contract_cols(jnp.concatenate(score_grads, axis=1), jnp.concatenate(q_parts, axis=1))
            * scale
        )
        value_grads.append(
            contract_cols(jnp.concatenate(probs, axis=1), jnp.concatenate(g_parts, axis=1))
        )
    kv_grad = jnp.concatenate(key_grads + value_grads, axis=1)
    before[...] = kv_grad[:WINDOW].astype(jnp.bfloat16)
    own[...] = kv_grad[WINDOW:]


def mix_body(high, low, expert_out, resid, out):
    mixed = jnp.dot(high[...], expert_out[...], preferred_element_type=jnp.float32)
    mixed = mixed + jnp.dot(low[...], expert_out[...], preferred_element_type=jnp.float32)
    value = resid[...].astype(jnp.float32) + mixed
    for start in range(0, D, 128):
        last = min(D, start + 128)
        out[start:last, :] = value[:, start:last].T.astype(jnp.bfloat16)


def per_device(
    hidden_in,
    query_proj,
    key_proj,
    value_proj,
    sink_logits,
    out_weight,
    norm_gain,
    expert_ids,
    gate_weights,
    gate_proj,
    up_proj,
    down_proj,
    out_grad,
):
    ctx_size = lax.axis_size("ctx")
    exp_size = lax.axis_size("exp")
    exp_index = lax.axis_index("exp")
    device = lax.axis_index("ctx") * exp_size + exp_index
    tok_dev = hidden_in.shape[0]
    first_row = device * tok_dev
    group = HQ // KVH
    scale = DH ** (-0.5)
    stride = min(512, tok_dev)
    experts = ctx_size * exp_size // 2
    capacity = tok_dev * TOPK // experts
    above, below, across = near_blocks(out_weight)
    kv_rows = jnp.concatenate([key_proj, value_proj], axis=1)
    earlier = from_behind(kv_rows, ("ctx", "exp"), 1)
    above, below, across, earlier = lax.optimization_barrier((above, below, across, earlier))
    up, down, over, up_over, down_over = far_blocks(above, below, across)
    where = jnp.stack([exp_index // 8, (exp_index // 2) % 4]).astype(jnp.int32)
    extended = jnp.concatenate([earlier, kv_rows], axis=0)
    core = exp_index % 2
    queries = query_proj.reshape(tok_dev, HQ, DH)
    by_head = extended.reshape(tok_dev + WINDOW, 2, KVH, DH)
    head_keys, head_values = (by_rows(by_head[:, kind].transpose(1, 0, 2)) for kind in range(2))
    head_turned = by_rows(by_head[:, 0].transpose(1, 2, 0))
    queries_turned = by_rows(query_proj.T)

    def operands(start, kv_head):
        q_rows = queries[start : start + stride, kv_head * group : (kv_head + 1) * group]
        key_span = extended[start : start + stride + WINDOW, kv_head * DH : (kv_head + 1) * DH]
        value_rows = extended[
            start : start + stride + WINDOW, (KVH + kv_head) * DH : (KVH + kv_head + 1) * DH
        ]
        return (q_rows, key_span, value_rows)

    def scores_of(q_rows, key_span, start):
        allowed = band_mask(first_row + start, stride)
        scores = (
            jnp.einsum("thd,jd->htj", q_rows, key_span, preferred_element_type=jnp.float32) * scale
        )
        return jnp.where(allowed[None], scores, NEG)

    start = 0
    head_outs = []
    span_stats = []
    for kv_head in range(KVH):
        q_rows, key_span, value_rows = operands(start, kv_head)
        scores = scores_of(q_rows, key_span, start)
        sinks = sink_logits[kv_head * group : (kv_head + 1) * group][:, None]
        peak = jnp.maximum(jnp.max(scores, axis=2), sinks)
        weights = jnp.exp(scores - peak[:, :, None])
        total = jnp.sum(weights, axis=2) + jnp.exp(sinks - peak)
        summed = jnp.einsum(
            "htj,jd->thd",
            weights.astype(jnp.bfloat16),
            value_rows,
            preferred_element_type=jnp.float32,
        )
        head_outs.append(summed / total.T[:, :, None])
        span_stats.append((peak, total))
    stats = [span_stats]
    out_rows = jnp.concatenate(head_outs, axis=1)
    attn = out_rows.reshape(tok_dev, HQ * DH).astype(jnp.bfloat16)
    targets = slot_targets(expert_ids, experts, capacity)
    slot_table = jnp.arange(experts * capacity, dtype=jnp.int32)
    picks = (targets[:, :, None] == slot_table[None, None, :]).astype(jnp.bfloat16)
    placed = jnp.sum(picks, axis=1)
    grad_f = out_grad.astype(jnp.float32)
    slot_weight = jnp.sum(gate_weights[:, :, None] * picks.astype(jnp.float32), axis=(0, 1))
    grad_slots = (slot_weight[:, None] * contract_rows(placed, out_grad)).astype(jnp.bfloat16)
    grad_slots = by_rows(grad_slots)
    over, up_over, down_over, grad_slots = lax.optimization_barrier(
        (over, up_over, down_over, grad_slots)
    )
    by_place = attn.reshape(tok_dev, 8, 2, 2 * DH)
    first, second = by_place[:, :, 0], by_place[:, :, 1]
    theirs = send(jnp.where(core == 0, second, first), TO_PEER).reshape(tok_dev, HQ * DH // 2)
    mine = jnp.where(core == 0, first, second).reshape(tok_dev, HQ * DH // 2)
    joined, for_peer, for_own = collect(
        where,
        (out_weight, above, below, across, up, down, over, up_over, down_over),
        jnp.concatenate([theirs.T, mine.T], axis=1),
    )
    attn_out = for_own.T + send(for_peer.T, TO_PEER)
    resid = lax.optimization_barrier(
        (hidden_in.astype(jnp.float32) + attn_out).astype(jnp.bfloat16)
    )
    resid = by_columns(resid)
    resid_f = resid.astype(jnp.float32)
    inv_rms = lax.rsqrt(jnp.mean(resid_f * resid_f, axis=1, keepdims=True) + EPS)
    normed = (resid_f * inv_rms * norm_gain).astype(jnp.bfloat16)
    def exchange(slots):
        return lax.all_to_all(
            slots.reshape(experts, capacity, D),
            AXES,
            split_axis=0,
            concat_axis=0,
            tiled=True,
            axis_index_groups=CORE_GROUPS,
        )

    def swap(value):
        return send(by_rows(value.reshape(experts, capacity, D)), TO_PEER)

    def flat(value):
        return by_rows(by_rows(value).reshape(experts * capacity, D))

    def add_halves(own, received):
        return (own.astype(jnp.float32) + received.astype(jnp.float32)).astype(jnp.bfloat16)

    w_gate = gate_proj[0]
    w_up = up_proj[0]
    w_down = down_proj[0]
    grads_own = exchange(grad_slots)
    grads_peer = flat(swap(grads_own))
    act_grad_own = by_columns(contract_cols(flat(grads_own), w_down))
    act_grad_peer = by_columns(contract_cols(grads_peer, w_down))

    slots_in = contract_rows(placed, normed).astype(jnp.bfloat16)
    early = (head_keys, head_values, head_turned, queries_turned, by_rows(resid), by_rows(out_grad))
    rows_own, act_grad_own, act_grad_peer, early = lax.optimization_barrier(
        (exchange(by_rows(slots_in)), act_grad_own, act_grad_peer, early)
    )
    head_keys, head_values, head_turned, queries_turned, resid_rows, grad_rows = early
    rows_peer = flat(swap(rows_own))
    rows_own = flat(rows_own)

    def hidden_units(rows, act_grad):
        gate_act = jnp.dot(rows, w_gate, preferred_element_type=jnp.float32)
        up_act = jnp.dot(rows, w_up, preferred_element_type=jnp.float32)
        sig = jax.nn.sigmoid(ALPHA * gate_act)
        act = (gate_act * sig * (up_act + 1.0)).astype(jnp.bfloat16)
        gate_grad = (
            act_grad * (up_act + 1.0) * sig * (1.0 + ALPHA * gate_act * (1.0 - sig))
        ).astype(jnp.bfloat16)
        up_grad = (act_grad * gate_act * sig).astype(jnp.bfloat16)
        return act, gate_grad, up_grad

    def row_grad_of(gate_grad, up_grad):
        return (contract_cols(gate_grad, w_gate) + contract_cols(up_grad, w_up)).astype(jnp.bfloat16)

    act_own, gate_grad_own, up_grad_own = hidden_units(rows_own, act_grad_own)
    rows_peer, act_own, gate_grad_own, up_grad_own = lax.optimization_barrier(
        (rows_peer, act_own, gate_grad_own, up_grad_own)
    )
    act_peer, gate_grad_peer, up_grad_peer = hidden_units(rows_peer, act_grad_peer)
    row_grad_peer = flat(swap(by_rows(row_grad_of(gate_grad_peer, up_grad_peer))))
    row_grad_own = lax.optimization_barrier(by_rows(row_grad_of(gate_grad_own, up_grad_own)))
    row_grad = by_rows(add_halves(row_grad_own, row_grad_peer))
    row_grad, act_own, act_peer = lax.optimization_barrier((row_grad, act_own, act_peer))
    normed_slots = flat(exchange(row_grad))
    rows_shape = jax.ShapeDtypeStruct((experts * capacity, D), jnp.bfloat16)
    part_peer = in_vmem(down_body, rows_shape, by_columns(act_peer).T, w_down)
    part_peer = by_rows(part_peer.reshape(experts, capacity, D))
    part_peer = [
        by_rows(by_rows(send(part, TO_PEER)).reshape(-1, D)) for part in jnp.split(part_peer, 4)
    ]
    part_sum = in_vmem(down_add_body, rows_shape, by_columns(act_own).T, w_down, *part_peer)
    normed_slots, part_sum = lax.optimization_barrier((normed_slots, part_sum))
    expert_out = flat(exchange(part_sum))

    combine = jnp.sum(gate_weights[:, :, None] * picks.astype(jnp.float32), axis=1)
    combine_high = combine.astype(jnp.bfloat16)
    combine_low = (combine - combine_high.astype(jnp.float32)).astype(jnp.bfloat16)
    layer_out = in_vmem(
        mix_body,
        jax.ShapeDtypeStruct((D, tok_dev), jnp.bfloat16),
        combine_high,
        combine_low,
        expert_out,
        resid_rows,
    ).T
    resid_grad = in_vmem(
        resid_grad_body,
        jax.ShapeDtypeStruct((tok_dev, D), jnp.bfloat16),
        placed,
        normed_slots,
        resid_rows,
        grad_rows,
        inv_rms,
        norm_gain.reshape(1, D),
    )
    peer_grad = send(resid_grad.reshape(tok_dev // 8, 8, D), TO_PEER).reshape(tok_dev, D)

    def attn_grad_of(value):
        return in_vmem(
            attn_grad_body,
            jax.ShapeDtypeStruct((HQ * DH // 2, tok_dev), jnp.bfloat16),
            value,
            joined,
            scalars=where,
        ).reshape(8, 2 * DH, tok_dev)

    grad_mine = attn_grad_of(resid_grad)
    grad_back = send(attn_grad_of(peer_grad), TO_PEER)
    attn_grad = jnp.where(
        core == 0,
        jnp.stack([grad_mine, grad_back], axis=1),
        jnp.stack([grad_back, grad_mine], axis=1),
    ).reshape(HQ * DH, tok_dev)
    smem, vmem = (pl.BlockSpec(memory_space=space) for space in (pltpu.SMEM, pltpu.VMEM))
    query_grad, before, own = pl.pallas_call(
        attn_back_body,
        out_shape=[
            jax.ShapeDtypeStruct((tok_dev, HQ * DH), jnp.bfloat16),
            jax.ShapeDtypeStruct((WINDOW, 2 * KVH * DH), jnp.bfloat16),
            jax.ShapeDtypeStruct((tok_dev, 2 * KVH * DH), jnp.float32),
        ],
        in_specs=[smem, smem] + [vmem] * 5,
        out_specs=[vmem] * 3,
        compiler_params=pltpu.CompilerParams(vmem_limit_bytes=24 * 1024 * 1024),
        cost_estimate=pl.CostEstimate(flops=1000, bytes_accessed=1000, transcendentals=0),
    )(
        (device == 0).astype(jnp.int32).reshape(1),
        sink_logits,
        queries_turned,
        attn_grad,
        head_keys,
        head_turned,
        head_values,
    )
    returned = from_behind(before, ("ctx", "exp"), -1).astype(jnp.float32)
    own = own + returned
    key_grad = own[:, : KVH * DH].astype(jnp.bfloat16)
    value_grad = own[:, KVH * DH :].astype(jnp.bfloat16)
    return (layer_out, resid_grad, query_grad, key_grad, value_grad)


def solution(mesh):
    in_specs = (
        P(("ctx", "exp"), None),
        P(("ctx", "exp"), None),
        P(("ctx", "exp"), None),
        P(("ctx", "exp"), None),
        P(),
        P("exp", None),
        P(),
        P(("ctx", "exp"), None),
        P(("ctx", "exp"), None),
        P(("ctx", "exp"), None, None),
        P(("ctx", "exp"), None, None),
        P(("ctx", "exp"), None, None),
        P(("ctx", "exp"), None),
    )
    out_specs = (
        P(("ctx", "exp"), None),
        P(("ctx", "exp"), None),
        P(("ctx", "exp"), None),
        P(("ctx", "exp"), None),
        P(("ctx", "exp"), None),
    )
    return jax.shard_map(
        per_device, mesh=mesh, in_specs=in_specs, out_specs=out_specs, check_vma=False
    )
```

```python
import jax
import jax.numpy as jnp
from jax import lax
from jax.experimental import pallas as pl
from jax.experimental.layout import Layout, with_layout_constraint
from jax.experimental.pallas import tpu as pltpu
from jax.sharding import PartitionSpec as P

D = 2880
HQ = 32
KVH = 4
DH = 64
TOPK = 4
WINDOW = 128


NEG = -1e30
EPS = 1e-05
ALPHA = 1.702


def from_behind(value, axis, steps):
    count = lax.axis_size(axis)
    initial, last = (max(0, -steps), min(count, count - steps))
    return lax.ppermute(value, axis, [(source, source + steps) for source in range(initial, last)])


def band_mask(first, count):
    query_pos = first + jnp.arange(count, dtype=jnp.int32)
    key_pos = first - WINDOW + jnp.arange(count + WINDOW, dtype=jnp.int32)
    diff = query_pos[:, None] - key_pos[None, :]
    return (diff >= 0) & (diff < WINDOW) & (key_pos[None, :] >= 0)


def slot_targets(expert_ids, experts, capacity):
    flat = expert_ids.reshape(-1)
    table = jnp.arange(experts, dtype=jnp.int32)
    hits = (flat[:, None] == table[None, :]).astype(jnp.int32)
    before = jnp.cumsum(hits, axis=0) - hits
    slot = jnp.sum(before * hits, axis=1)
    return (flat * capacity + slot).reshape(expert_ids.shape)


def place(z_lo, x, z_hi, y, core):
    return (z_lo * 4 + x) * 16 + z_hi * 8 + y * 2 + core


def moves(step):
    pairs = []
    for source in range(128):
        outer, inner = divmod(source, 16)
        z_lo, x = divmod(outer, 4)
        z_hi, rest = divmod(inner, 8)
        y, core = divmod(rest, 2)
        x2, y2, z2, core2 = step(x, y, z_hi * 2 + z_lo, core)
        pairs.append((source, place(z2 % 2, x2 % 4, z2 // 2, y2 % 4, core2)))
    return pairs


AXES = ("ctx", "exp")
TO_PEER = moves(lambda x, y, z, core: (x, y, z, 1 - core))
TO_HIGH_Y = moves(lambda x, y, z, core: (x, y + 1, z, core))
TO_LOW_Y = moves(lambda x, y, z, core: (x, y - 1, z, core))
ACROSS_Z = moves(lambda x, y, z, core: (x, y, 3 - z, core))
HIGH_Y_ACROSS = moves(lambda x, y, z, core: (x, y + 1, 3 - z, core))
LOW_Y_ACROSS = moves(lambda x, y, z, core: (x, y - 1, 3 - z, core))
CORE_GROUPS = [list(range(0, 128, 2)), list(range(1, 128, 2))]


def send(value, pairs):
    return lax.ppermute(value, AXES, pairs)


def by_rows(value):
    return with_layout_constraint(value, Layout(tuple(range(value.ndim))))


def by_columns(value):
    return with_layout_constraint(value, Layout((1, 0)))


OVER = D // 4


def near_blocks(block):
    return send(block, TO_LOW_Y), send(block, TO_HIGH_Y), send(block, ACROSS_Z)


def far_blocks(above, below, across):
    part, rest, half = OVER, D - OVER, D // 2
    up = send(jnp.concatenate([across[:, part:], below[:, :half]], axis=1), TO_HIGH_Y)
    down = send(jnp.concatenate([across[:, :rest], above[:, half:]], axis=1), TO_LOW_Y)
    over = send(jnp.concatenate([below[:, :part], above[:, rest:]], axis=1), ACROSS_Z)
    up_over = send(below[:, :half], HIGH_Y_ACROSS)
    down_over = send(above[:, half:], LOW_Y_ACROSS)
    return up, down, over, up_over, down_over


REST, HALF_D = D - OVER, D // 2
SOURCES = {
    0: [(0, D, 0, 0)],
    1: [(0, D, 1, 0)],
    3: [(0, D, 2, 0)],
    4: [(0, D, 3, 0)],
    7: [(0, OVER, 6, 0), (OVER, REST, 4, 0)],
    2: [(0, HALF_D, 4, REST), (HALF_D, HALF_D, 5, REST)],
    5: [(0, REST, 5, 0), (REST, OVER, 6, OVER)],
    6: [(0, HALF_D, 7, 0), (HALF_D, HALF_D, 8, 0)],
}


def place_of(where, place):
    z_hi = (where[0] + place // 4) % 2
    return z_hi * 4 + (where[1] + place % 4) % 4


def collect_body(where, *refs):
    *parts, columns, joined, for_peer, for_own = refs
    rows = parts[0].shape[1]
    picked = jnp.concatenate(
        [columns[pl.ds(place_of(where, place) * rows, rows), :] for place in range(8)], axis=0
    )
    edges = (0, OVER, HALF_D, REST, D)
    for first, last in zip(edges[:-1], edges[1:]):
        found = []
        for place in range(8):
            for start, count, index, offset in SOURCES[place]:
                if start <= first and last <= start + count:
                    at = offset + first - start
                    found.append(parts[index][at : at + last - first, :])
        side = jnp.concatenate(found, axis=1)
        joined[first:last, :] = side
        product = jnp.dot(side, picked, preferred_element_type=jnp.float32)
        for_peer[first:last, :] = product[:, :rows]
        for_own[first:last, :] = product[:, rows:]


def collect(where, parts, columns):
    product = jax.ShapeDtypeStruct((D, columns.shape[1] // 2), jnp.float32)
    return in_vmem(
        collect_body,
        [jax.ShapeDtypeStruct((D, columns.shape[0]), jnp.bfloat16), product, product],
        *[part.T for part in parts],
        columns,
        scalars=where,
        mib=24,
    )


def contract_rows(left, right):
    return lax.dot_general(
        left, right, (((0,), (0,)), ((), ())), preferred_element_type=jnp.float32
    )


def contract_cols(left, right):
    return lax.dot_general(
        left, right, (((1,), (1,)), ((), ())), preferred_element_type=jnp.float32
    )


def in_vmem(body, out_shape, *operands, scalars=None, mib=16):
    spec = pl.BlockSpec(memory_space=pltpu.VMEM)
    in_specs = [spec] * len(operands)
    if scalars is not None:
        in_specs = [pl.BlockSpec(memory_space=pltpu.SMEM)] + in_specs
        operands = (scalars, *operands)
    return pl.pallas_call(
        body,
        out_shape=out_shape,
        in_specs=in_specs,
        out_specs=jax.tree.map(lambda _: spec, out_shape),
        compiler_params=pltpu.CompilerParams(vmem_limit_bytes=mib * 1024 * 1024),
        cost_estimate=pl.CostEstimate(flops=1000, bytes_accessed=1000, transcendentals=0),
    )(*operands)


def resid_grad_body(placed, slots, resid, grad, inv_rms, gain, out):
    normed_grad = jnp.dot(placed[...], slots[...], preferred_element_type=jnp.float32)
    scaled = gain[...] * normed_grad
    resid_f = resid[...].astype(jnp.float32)
    inv = inv_rms[...]
    inner = jnp.sum(resid_f * scaled, axis=1, keepdims=True) * (1.0 / D)
    value = grad[...].astype(jnp.float32) + inv * scaled - resid_f * (inv * inv * inv) * inner
    out[...] = value.astype(jnp.bfloat16)


def attn_grad_body(where, resid_grad, projection, out):
    rows = resid_grad.shape[0]
    grad = jnp.dot(resid_grad[...], projection[...], preferred_element_type=jnp.float32).T
    for place in range(8):
        out[pl.ds(place_of(where, place) * rows, rows), :] = grad[
            place * rows : (place + 1) * rows
        ].astype(jnp.bfloat16)


def copy_body(source, out):
    out[...] = source[...]


def down_body(act, weight, out):
    out[...] = contract_rows(act[...], weight[...]).astype(jnp.bfloat16)


def down_add_body(act, weight, *refs):
    *quarters, out = refs
    rows = act.shape[1] // len(quarters)
    for number, received in enumerate(quarters):
        at = pl.ds(number * rows, rows)
        own = contract_rows(act[:, at], weight[...])
        own = own.astype(jnp.bfloat16).astype(jnp.float32)
        out[at, :] = (own + received[...].astype(jnp.float32)).astype(jnp.bfloat16)


def attn_back_body(first_block, sinks, queries, grads, keys, turned, values, dq, before, own):
    tokens = queries.shape[1]
    span = keys.shape[1]
    key_at = lax.broadcasted_iota(jnp.int32, (span, 2 * tokens), 0)
    lane = lax.broadcasted_iota(jnp.int32, (1, 2 * tokens), 1)
    token = lax.rem(lane, tokens)
    allowed = (key_at > token) & (key_at <= token + WINDOW)
    allowed = allowed & (key_at >= WINDOW * first_block[0])
    scale = DH ** (-0.5)
    group = HQ // KVH

    def two_heads(ref, head):
        return jnp.concatenate(
            [ref[head * DH : (head + 1) * DH, :], ref[(head + 1) * DH : (head + 2) * DH, :]], axis=1
        )

    key_grads, value_grads = [], []
    for kv_head in range(KVH):
        key_rows, value_rows, key_columns = keys[kv_head], values[kv_head], turned[kv_head]
        score_grads, probs, q_parts, g_parts = [], [], [], []
        for head in range(kv_head * group, (kv_head + 1) * group, 2):
            q, g = two_heads(queries, head), two_heads(grads, head)
            scores = jnp.dot(key_rows, q, preferred_element_type=jnp.float32) * scale
            scores = jnp.where(allowed, scores, NEG)
            sink = jnp.where(lane < tokens, sinks[head], sinks[head + 1])
            peak = jnp.maximum(jnp.max(scores, axis=0, keepdims=True), sink)
            weights = jnp.exp(scores - peak)
            total = jnp.sum(weights, axis=0, keepdims=True) + jnp.exp(sink - peak)
            inverse = 1.0 / total
            prob_grad = jnp.dot(value_rows, g, preferred_element_type=jnp.float32)
            rounded = weights.astype(jnp.bfloat16).astype(jnp.float32)
            delta = jnp.sum(rounded * prob_grad, axis=0, keepdims=True) * inverse
            prob = weights * inverse
            score_grad = (prob * (prob_grad - delta)).astype(jnp.bfloat16)
            turned_dq = jnp.dot(key_columns, score_grad, preferred_element_type=jnp.float32) * scale
            both = jnp.concatenate([turned_dq[:, :tokens], turned_dq[:, tokens:]], axis=0)
            dq[:, head * DH : (head + 2) * DH] = both.T.astype(jnp.bfloat16)
            score_grads.append(score_grad)
            probs.append(prob.astype(jnp.bfloat16))
            q_parts.append(q)
            g_parts.append(g)
        key_grads.append(
            contract_cols(jnp.concatenate(score_grads, axis=1), jnp.concatenate(q_parts, axis=1))
            * scale
        )
        value_grads.append(
            contract_cols(jnp.concatenate(probs, axis=1), jnp.concatenate(g_parts, axis=1))
        )
    kv_grad = jnp.concatenate(key_grads + value_grads, axis=1)
    before[...] = kv_grad[:WINDOW].astype(jnp.bfloat16)
    own[...] = kv_grad[WINDOW:]


def mix_body(high, low, expert_out, resid, out):
    mixed = jnp.dot(high[...], expert_out[...], preferred_element_type=jnp.float32)
    mixed = mixed + jnp.dot(low[...], expert_out[...], preferred_element_type=jnp.float32)
    value = resid[...].astype(jnp.float32) + mixed
    for start in range(0, D, 128):
        last = min(D, start + 128)
        out[start:last, :] = value[:, start:last].T.astype(jnp.bfloat16)


def per_device(
    hidden_in,
    query_proj,
    key_proj,
    value_proj,
    sink_logits,
    out_weight,
    norm_gain,
    expert_ids,
    gate_weights,
    gate_proj,
    up_proj,
    down_proj,
    out_grad,
):
    ctx_size = lax.axis_size("ctx")
    exp_size = lax.axis_size("exp")
    exp_index = lax.axis_index("exp")
    device = lax.axis_index("ctx") * exp_size + exp_index
    tok_dev = hidden_in.shape[0]
    first_row = device * tok_dev
    group = HQ // KVH
    scale = DH ** (-0.5)
    stride = min(512, tok_dev)
    experts = ctx_size * exp_size // 2
    capacity = tok_dev * TOPK // experts
    above, below, across = near_blocks(out_weight)
    kv_rows = jnp.concatenate([key_proj, value_proj], axis=1)
    earlier = from_behind(kv_rows, ("ctx", "exp"), 1)
    above, below, across, earlier = lax.optimization_barrier((above, below, across, earlier))
    up, down, over, up_over, down_over = far_blocks(above, below, across)
    where = jnp.stack([exp_index // 8, (exp_index // 2) % 4]).astype(jnp.int32)
    extended = jnp.concatenate([earlier, kv_rows], axis=0)
    core = exp_index % 2
    queries = query_proj.reshape(tok_dev, HQ, DH)
    by_head = extended.reshape(tok_dev + WINDOW, 2, KVH, DH)
    head_keys, head_values = (by_rows(by_head[:, kind].transpose(1, 0, 2)) for kind in range(2))
    head_turned = by_rows(by_head[:, 0].transpose(1, 2, 0))
    queries_turned = by_rows(query_proj.T)

    def operands(start, kv_head):
        q_rows = queries[start : start + stride, kv_head * group : (kv_head + 1) * group]
        key_span = extended[start : start + stride + WINDOW, kv_head * DH : (kv_head + 1) * DH]
        value_rows = extended[
            start : start + stride + WINDOW, (KVH + kv_head) * DH : (KVH + kv_head + 1) * DH
        ]
        return (q_rows, key_span, value_rows)

    def scores_of(q_rows, key_span, start):
        allowed = band_mask(first_row + start, stride)
        scores = (
            jnp.einsum("thd,jd->htj", q_rows, key_span, preferred_element_type=jnp.float32) * scale
        )
        return jnp.where(allowed[None], scores, NEG)

    start = 0
    head_outs = []
    span_stats = []
    for kv_head in range(KVH):
        q_rows, key_span, value_rows = operands(start, kv_head)
        scores = scores_of(q_rows, key_span, start)
        sinks = sink_logits[kv_head * group : (kv_head + 1) * group][:, None]
        peak = jnp.maximum(jnp.max(scores, axis=2), sinks)
        weights = jnp.exp(scores - peak[:, :, None])
        total = jnp.sum(weights, axis=2) + jnp.exp(sinks - peak)
        summed = jnp.einsum(
            "htj,jd->thd",
            weights.astype(jnp.bfloat16),
            value_rows,
            preferred_element_type=jnp.float32,
        )
        head_outs.append(summed / total.T[:, :, None])
        span_stats.append((peak, total))
    stats = [span_stats]
    out_rows = jnp.concatenate(head_outs, axis=1)
    attn = out_rows.reshape(tok_dev, HQ * DH).astype(jnp.bfloat16)
    targets = slot_targets(expert_ids, experts, capacity)
    slot_table = jnp.arange(experts * capacity, dtype=jnp.int32)
    picks = (targets[:, :, None] == slot_table[None, None, :]).astype(jnp.bfloat16)
    placed = jnp.sum(picks, axis=1)
    grad_f = out_grad.astype(jnp.float32)
    slot_weight = jnp.sum(gate_weights[:, :, None] * picks.astype(jnp.float32), axis=(0, 1))
    grad_slots = (slot_weight[:, None] * contract_rows(placed, out_grad)).astype(jnp.bfloat16)
    grad_slots = by_rows(grad_slots)
    over, up_over, down_over, grad_slots = lax.optimization_barrier(
        (over, up_over, down_over, grad_slots)
    )
    by_place = attn.reshape(tok_dev, 8, 2, 2 * DH)
    first, second = by_place[:, :, 0], by_place[:, :, 1]
    theirs = send(jnp.where(core == 0, second, first), TO_PEER).reshape(tok_dev, HQ * DH // 2)
    mine = jnp.where(core == 0, first, second).reshape(tok_dev, HQ * DH // 2)
    joined, for_peer, for_own = collect(
        where,
        (out_weight, above, below, across, up, down, over, up_over, down_over),
        jnp.concatenate([theirs.T, mine.T], axis=1),
    )
    attn_out = for_own.T + send(for_peer.T, TO_PEER)
    resid = lax.optimization_barrier(
        (hidden_in.astype(jnp.float32) + attn_out).astype(jnp.bfloat16)
    )
    resid = by_columns(resid)
    resid_f = resid.astype(jnp.float32)
    inv_rms = lax.rsqrt(jnp.mean(resid_f * resid_f, axis=1, keepdims=True) + EPS)
    normed = (resid_f * inv_rms * norm_gain).astype(jnp.bfloat16)
    def exchange(slots):
        return lax.all_to_all(
            slots.reshape(experts, capacity, D),
            AXES,
            split_axis=0,
            concat_axis=0,
            tiled=True,
            axis_index_groups=CORE_GROUPS,
        )

    def swap(value):
        return send(by_rows(value.reshape(experts, capacity, D)), TO_PEER)

    def flat(value):
        return by_rows(by_rows(value).reshape(experts * capacity, D))

    def add_halves(own, received):
        return (own.astype(jnp.float32) + received.astype(jnp.float32)).astype(jnp.bfloat16)

    w_gate = gate_proj[0]
    w_up = up_proj[0]
    w_down = down_proj[0]
    grads_own = exchange(grad_slots)
    grads_peer = flat(swap(grads_own))
    act_grad_own = by_columns(contract_cols(flat(grads_own), w_down))
    act_grad_peer = by_columns(contract_cols(grads_peer, w_down))

    slots_in = contract_rows(placed, normed).astype(jnp.bfloat16)
    early = (head_keys, head_values, head_turned, queries_turned, by_rows(resid), by_rows(out_grad))
    rows_own, act_grad_own, act_grad_peer, early = lax.optimization_barrier(
        (exchange(by_rows(slots_in)), act_grad_own, act_grad_peer, early)
    )
    head_keys, head_values, head_turned, queries_turned, resid_rows, grad_rows = early
    rows_peer = flat(swap(rows_own))
    rows_own = in_vmem(
        copy_body, jax.ShapeDtypeStruct((experts * capacity, D), jnp.bfloat16), flat(rows_own)
    )

    def hidden_units(rows, act_grad):
        gate_act = jnp.dot(rows, w_gate, preferred_element_type=jnp.float32)
        up_act = jnp.dot(rows, w_up, preferred_element_type=jnp.float32)
        sig = jax.nn.sigmoid(ALPHA * gate_act)
        act = (gate_act * sig * (up_act + 1.0)).astype(jnp.bfloat16)
        gate_grad = (
            act_grad * (up_act + 1.0) * sig * (1.0 + ALPHA * gate_act * (1.0 - sig))
        ).astype(jnp.bfloat16)
        up_grad = (act_grad * gate_act * sig).astype(jnp.bfloat16)
        return act, gate_grad, up_grad

    def row_grad_of(gate_grad, up_grad):
        return (contract_cols(gate_grad, w_gate) + contract_cols(up_grad, w_up)).astype(jnp.bfloat16)

    act_own, gate_grad_own, up_grad_own = hidden_units(rows_own, act_grad_own)
    rows_peer, act_own, gate_grad_own, up_grad_own = lax.optimization_barrier(
        (rows_peer, act_own, gate_grad_own, up_grad_own)
    )
    act_peer, gate_grad_peer, up_grad_peer = hidden_units(rows_peer, act_grad_peer)
    row_grad_peer = flat(swap(by_rows(row_grad_of(gate_grad_peer, up_grad_peer))))
    row_grad_own = lax.optimization_barrier(by_rows(row_grad_of(gate_grad_own, up_grad_own)))
    row_grad = by_rows(add_halves(row_grad_own, row_grad_peer))
    row_grad, act_own, act_peer = lax.optimization_barrier((row_grad, act_own, act_peer))
    normed_slots = flat(exchange(row_grad))
    rows_shape = jax.ShapeDtypeStruct((experts * capacity, D), jnp.bfloat16)
    part_peer = in_vmem(down_body, rows_shape, by_columns(act_peer).T, w_down)
    part_peer = by_rows(part_peer.reshape(experts, capacity, D))
    part_peer = [
        by_rows(by_rows(send(part, TO_PEER)).reshape(-1, D)) for part in jnp.split(part_peer, 4)
    ]
    part_sum = in_vmem(down_add_body, rows_shape, by_columns(act_own).T, w_down, *part_peer)
    normed_slots, part_sum = lax.optimization_barrier((normed_slots, part_sum))
    expert_out = flat(exchange(part_sum))

    combine = jnp.sum(gate_weights[:, :, None] * picks.astype(jnp.float32), axis=1)
    combine_high = combine.astype(jnp.bfloat16)
    combine_low = (combine - combine_high.astype(jnp.float32)).astype(jnp.bfloat16)
    layer_out = in_vmem(
        mix_body,
        jax.ShapeDtypeStruct((D, tok_dev), jnp.bfloat16),
        combine_high,
        combine_low,
        expert_out,
        resid_rows,
    ).T
    resid_grad = in_vmem(
        resid_grad_body,
        jax.ShapeDtypeStruct((tok_dev, D), jnp.bfloat16),
        placed,
        normed_slots,
        resid_rows,
        grad_rows,
        inv_rms,
        norm_gain.reshape(1, D),
    )
    peer_grad = send(resid_grad.reshape(tok_dev // 8, 8, D), TO_PEER).reshape(tok_dev, D)

    def attn_grad_of(value):
        return in_vmem(
            attn_grad_body,
            jax.ShapeDtypeStruct((HQ * DH // 2, tok_dev), jnp.bfloat16),
            value,
            joined,
            scalars=where,
        ).reshape(8, 2 * DH, tok_dev)

    grad_mine = attn_grad_of(resid_grad)
    grad_back = send(attn_grad_of(peer_grad), TO_PEER)
    attn_grad = jnp.where(
        core == 0,
        jnp.stack([grad_mine, grad_back], axis=1),
        jnp.stack([grad_back, grad_mine], axis=1),
    ).reshape(HQ * DH, tok_dev)
    smem, vmem = (pl.BlockSpec(memory_space=space) for space in (pltpu.SMEM, pltpu.VMEM))
    query_grad, before, own = pl.pallas_call(
        attn_back_body,
        out_shape=[
            jax.ShapeDtypeStruct((tok_dev, HQ * DH), jnp.bfloat16),
            jax.ShapeDtypeStruct((WINDOW, 2 * KVH * DH), jnp.bfloat16),
            jax.ShapeDtypeStruct((tok_dev, 2 * KVH * DH), jnp.float32),
        ],
        in_specs=[smem, smem] + [vmem] * 5,
        out_specs=[vmem] * 3,
        compiler_params=pltpu.CompilerParams(vmem_limit_bytes=24 * 1024 * 1024),
        cost_estimate=pl.CostEstimate(flops=1000, bytes_accessed=1000, transcendentals=0),
    )(
        (device == 0).astype(jnp.int32).reshape(1),
        sink_logits,
        queries_turned,
        attn_grad,
        head_keys,
        head_turned,
        head_values,
    )
    returned = from_behind(before, ("ctx", "exp"), -1).astype(jnp.float32)
    own = own + returned
    key_grad = own[:, : KVH * DH].astype(jnp.bfloat16)
    value_grad = own[:, KVH * DH :].astype(jnp.bfloat16)
    return (layer_out, resid_grad, query_grad, key_grad, value_grad)


def solution(mesh):
    in_specs = (
        P(("ctx", "exp"), None),
        P(("ctx", "exp"), None),
        P(("ctx", "exp"), None),
        P(("ctx", "exp"), None),
        P(),
        P("exp", None),
        P(),
        P(("ctx", "exp"), None),
        P(("ctx", "exp"), None),
        P(("ctx", "exp"), None, None),
        P(("ctx", "exp"), None, None),
        P(("ctx", "exp"), None, None),
        P(("ctx", "exp"), None),
    )
    out_specs = (
        P(("ctx", "exp"), None),
        P(("ctx", "exp"), None),
        P(("ctx", "exp"), None),
        P(("ctx", "exp"), None),
        P(("ctx", "exp"), None),
    )
    return jax.shard_map(
        per_device, mesh=mesh, in_specs=in_specs, out_specs=out_specs, check_vma=False
    )
```

```python
import jax
import jax.numpy as jnp
from jax import lax
from jax.experimental import pallas as pl
from jax.experimental.layout import Layout, with_layout_constraint
from jax.experimental.pallas import tpu as pltpu
from jax.sharding import PartitionSpec as P

D = 2880
HQ = 32
KVH = 4
DH = 64
TOPK = 4
WINDOW = 128


NEG = -1e30
EPS = 1e-05
ALPHA = 1.702


def from_behind(value, axis, steps):
    count = lax.axis_size(axis)
    initial, last = (max(0, -steps), min(count, count - steps))
    return lax.ppermute(value, axis, [(source, source + steps) for source in range(initial, last)])


def band_mask(first, count):
    query_pos = first + jnp.arange(count, dtype=jnp.int32)
    key_pos = first - WINDOW + jnp.arange(count + WINDOW, dtype=jnp.int32)
    diff = query_pos[:, None] - key_pos[None, :]
    return (diff >= 0) & (diff < WINDOW) & (key_pos[None, :] >= 0)


def slot_targets(expert_ids, experts, capacity):
    flat = expert_ids.reshape(-1)
    table = jnp.arange(experts, dtype=jnp.int32)
    hits = (flat[:, None] == table[None, :]).astype(jnp.int32)
    before = jnp.cumsum(hits, axis=0) - hits
    slot = jnp.sum(before * hits, axis=1)
    return (flat * capacity + slot).reshape(expert_ids.shape)


def place(z_lo, x, z_hi, y, core):
    return (z_lo * 4 + x) * 16 + z_hi * 8 + y * 2 + core


def moves(step):
    pairs = []
    for source in range(128):
        outer, inner = divmod(source, 16)
        z_lo, x = divmod(outer, 4)
        z_hi, rest = divmod(inner, 8)
        y, core = divmod(rest, 2)
        x2, y2, z2, core2 = step(x, y, z_hi * 2 + z_lo, core)
        pairs.append((source, place(z2 % 2, x2 % 4, z2 // 2, y2 % 4, core2)))
    return pairs


AXES = ("ctx", "exp")
TO_PEER = moves(lambda x, y, z, core: (x, y, z, 1 - core))
TO_HIGH_Y = moves(lambda x, y, z, core: (x, y + 1, z, core))
TO_LOW_Y = moves(lambda x, y, z, core: (x, y - 1, z, core))
ACROSS_Z = moves(lambda x, y, z, core: (x, y, 3 - z, core))
HIGH_Y_ACROSS = moves(lambda x, y, z, core: (x, y + 1, 3 - z, core))
LOW_Y_ACROSS = moves(lambda x, y, z, core: (x, y - 1, 3 - z, core))
CORE_GROUPS = [list(range(0, 128, 2)), list(range(1, 128, 2))]


def send(value, pairs):
    return lax.ppermute(value, AXES, pairs)


def by_rows(value):
    return with_layout_constraint(value, Layout(tuple(range(value.ndim))))


def by_columns(value):
    return with_layout_constraint(value, Layout((1, 0)))


OVER = D // 4


def near_blocks(block):
    return send(block, TO_LOW_Y), send(block, TO_HIGH_Y), send(block, ACROSS_Z)


def far_blocks(above, below, across):
    part, rest, half = OVER, D - OVER, D // 2
    up = send(jnp.concatenate([across[:, part:], below[:, :half]], axis=1), TO_HIGH_Y)
    down = send(jnp.concatenate([across[:, :rest], above[:, half:]], axis=1), TO_LOW_Y)
    over = send(jnp.concatenate([below[:, :part], above[:, rest:]], axis=1), ACROSS_Z)
    up_over = send(below[:, :half], HIGH_Y_ACROSS)
    down_over = send(above[:, half:], LOW_Y_ACROSS)
    return up, down, over, up_over, down_over


REST, HALF_D = D - OVER, D // 2
SOURCES = {
    0: [(0, D, 0, 0)],
    1: [(0, D, 1, 0)],
    3: [(0, D, 2, 0)],
    4: [(0, D, 3, 0)],
    7: [(0, OVER, 6, 0), (OVER, REST, 4, 0)],
    2: [(0, HALF_D, 4, REST), (HALF_D, HALF_D, 5, REST)],
    5: [(0, REST, 5, 0), (REST, OVER, 6, OVER)],
    6: [(0, HALF_D, 7, 0), (HALF_D, HALF_D, 8, 0)],
}


def place_of(where, place):
    z_hi = (where[0] + place // 4) % 2
    return z_hi * 4 + (where[1] + place % 4) % 4


def collect_body(where, *refs):
    *parts, columns, joined, for_peer, for_own = refs
    rows = parts[0].shape[1]
    picked = jnp.concatenate(
        [columns[pl.ds(place_of(where, place) * rows, rows), :] for place in range(8)], axis=0
    )
    edges = (0, OVER, HALF_D, REST, D)
    for first, last in zip(edges[:-1], edges[1:]):
        found = []
        for place in range(8):
            for start, count, index, offset in SOURCES[place]:
                if start <= first and last <= start + count:
                    at = offset + first - start
                    found.append(parts[index][at : at + last - first, :])
        side = jnp.concatenate(found, axis=1)
        joined[first:last, :] = side
        product = jnp.dot(side, picked, preferred_element_type=jnp.float32)
        for_peer[first:last, :] = product[:, :rows]
        for_own[first:last, :] = product[:, rows:]


def collect(where, parts, columns):
    product = jax.ShapeDtypeStruct((D, columns.shape[1] // 2), jnp.float32)
    return in_vmem(
        collect_body,
        [jax.ShapeDtypeStruct((D, columns.shape[0]), jnp.bfloat16), product, product],
        *[part.T for part in parts],
        columns,
        scalars=where,
        mib=24,
    )


def contract_rows(left, right):
    return lax.dot_general(
        left, right, (((0,), (0,)), ((), ())), preferred_element_type=jnp.float32
    )


def contract_cols(left, right):
    return lax.dot_general(
        left, right, (((1,), (1,)), ((), ())), preferred_element_type=jnp.float32
    )


def in_vmem(body, out_shape, *operands, scalars=None, mib=16):
    spec = pl.BlockSpec(memory_space=pltpu.VMEM)
    in_specs = [spec] * len(operands)
    if scalars is not None:
        in_specs = [pl.BlockSpec(memory_space=pltpu.SMEM)] + in_specs
        operands = (scalars, *operands)
    return pl.pallas_call(
        body,
        out_shape=out_shape,
        in_specs=in_specs,
        out_specs=jax.tree.map(lambda _: spec, out_shape),
        compiler_params=pltpu.CompilerParams(vmem_limit_bytes=mib * 1024 * 1024),
        cost_estimate=pl.CostEstimate(flops=1000, bytes_accessed=1000, transcendentals=0),
    )(*operands)


def resid_grad_body(placed, slots, resid, grad, inv_rms, gain, out):
    normed_grad = jnp.dot(placed[...], slots[...], preferred_element_type=jnp.float32)
    scaled = gain[...] * normed_grad
    resid_f = resid[...].astype(jnp.float32)
    inv = inv_rms[...]
    inner = jnp.sum(resid_f * scaled, axis=1, keepdims=True) * (1.0 / D)
    value = grad[...].astype(jnp.float32) + inv * scaled - resid_f * (inv * inv * inv) * inner
    out[...] = value.astype(jnp.bfloat16)


def attn_grad_body(where, resid_grad, projection, out):
    rows = resid_grad.shape[0]
    grad = jnp.dot(resid_grad[...], projection[...], preferred_element_type=jnp.float32).T
    for place in range(8):
        out[pl.ds(place_of(where, place) * rows, rows), :] = grad[
            place * rows : (place + 1) * rows
        ].astype(jnp.bfloat16)


def copy_body(source, out):
    out[...] = source[...]


def down_body(act, weight, out):
    out[...] = contract_rows(act[...], weight[...]).astype(jnp.bfloat16)


def down_add_body(act, weight, *refs):
    *quarters, out = refs
    rows = act.shape[1] // len(quarters)
    for number, received in enumerate(quarters):
        at = pl.ds(number * rows, rows)
        own = contract_rows(act[:, at], weight[...])
        own = own.astype(jnp.bfloat16).astype(jnp.float32)
        out[at, :] = (own + received[...].astype(jnp.float32)).astype(jnp.bfloat16)


def attn_back_body(first_block, sinks, queries, grads, keys, turned, values, dq, before, own):
    tokens = queries.shape[1]
    span = keys.shape[1]
    key_at = lax.broadcasted_iota(jnp.int32, (span, 2 * tokens), 0)
    lane = lax.broadcasted_iota(jnp.int32, (1, 2 * tokens), 1)
    token = lax.rem(lane, tokens)
    allowed = (key_at > token) & (key_at <= token + WINDOW)
    allowed = allowed & (key_at >= WINDOW * first_block[0])
    scale = DH ** (-0.5)
    group = HQ // KVH

    def two_heads(ref, head):
        return jnp.concatenate(
            [ref[head * DH : (head + 1) * DH, :], ref[(head + 1) * DH : (head + 2) * DH, :]], axis=1
        )

    key_grads, value_grads = [], []
    for kv_head in range(KVH):
        key_rows, value_rows, key_columns = keys[kv_head], values[kv_head], turned[kv_head]
        score_grads, probs, q_parts, g_parts = [], [], [], []
        for head in range(kv_head * group, (kv_head + 1) * group, 2):
            q, g = two_heads(queries, head), two_heads(grads, head)
            scores = jnp.dot(key_rows, q, preferred_element_type=jnp.float32) * scale
            scores = jnp.where(allowed, scores, NEG)
            sink = jnp.where(lane < tokens, sinks[head], sinks[head + 1])
            peak = jnp.maximum(jnp.max(scores, axis=0, keepdims=True), sink)
            weights = jnp.exp(scores - peak)
            total = jnp.sum(weights, axis=0, keepdims=True) + jnp.exp(sink - peak)
            inverse = 1.0 / total
            prob_grad = jnp.dot(value_rows, g, preferred_element_type=jnp.float32)
            rounded = weights.astype(jnp.bfloat16).astype(jnp.float32)
            delta = jnp.sum(rounded * prob_grad, axis=0, keepdims=True) * inverse
            prob = weights * inverse
            score_grad = (prob * (prob_grad - delta)).astype(jnp.bfloat16)
            turned_dq = jnp.dot(key_columns, score_grad, preferred_element_type=jnp.float32) * scale
            both = jnp.concatenate([turned_dq[:, :tokens], turned_dq[:, tokens:]], axis=0)
            dq[:, head * DH : (head + 2) * DH] = both.T.astype(jnp.bfloat16)
            score_grads.append(score_grad)
            probs.append(prob.astype(jnp.bfloat16))
            q_parts.append(q)
            g_parts.append(g)
        key_grads.append(
            contract_cols(jnp.concatenate(score_grads, axis=1), jnp.concatenate(q_parts, axis=1))
            * scale
        )
        value_grads.append(
            contract_cols(jnp.concatenate(probs, axis=1), jnp.concatenate(g_parts, axis=1))
        )
    kv_grad = jnp.concatenate(key_grads + value_grads, axis=1)
    before[...] = kv_grad[:WINDOW].astype(jnp.bfloat16)
    own[...] = kv_grad[WINDOW:]


def mix_body(high, low, expert_out, resid, out):
    mixed = jnp.dot(high[...], expert_out[...], preferred_element_type=jnp.float32)
    mixed = mixed + jnp.dot(low[...], expert_out[...], preferred_element_type=jnp.float32)
    value = resid[...].astype(jnp.float32) + mixed
    for start in range(0, D, 128):
        last = min(D, start + 128)
        out[start:last, :] = value[:, start:last].T.astype(jnp.bfloat16)


def per_device(
    hidden_in,
    query_proj,
    key_proj,
    value_proj,
    sink_logits,
    out_weight,
    norm_gain,
    expert_ids,
    gate_weights,
    gate_proj,
    up_proj,
    down_proj,
    out_grad,
):
    ctx_size = lax.axis_size("ctx")
    exp_size = lax.axis_size("exp")
    exp_index = lax.axis_index("exp")
    device = lax.axis_index("ctx") * exp_size + exp_index
    tok_dev = hidden_in.shape[0]
    first_row = device * tok_dev
    group = HQ // KVH
    scale = DH ** (-0.5)
    stride = min(512, tok_dev)
    experts = ctx_size * exp_size // 2
    capacity = tok_dev * TOPK // experts
    above, below, across = near_blocks(out_weight)
    kv_rows = jnp.concatenate([key_proj, value_proj], axis=1)
    earlier = from_behind(kv_rows, ("ctx", "exp"), 1)
    above, below, across, earlier = lax.optimization_barrier((above, below, across, earlier))
    up, down, over, up_over, down_over = far_blocks(above, below, across)
    where = jnp.stack([exp_index // 8, (exp_index // 2) % 4]).astype(jnp.int32)
    extended = jnp.concatenate([earlier, kv_rows], axis=0)
    core = exp_index % 2
    queries = query_proj.reshape(tok_dev, HQ, DH)
    by_head = extended.reshape(tok_dev + WINDOW, 2, KVH, DH)
    head_keys, head_values = (by_rows(by_head[:, kind].transpose(1, 0, 2)) for kind in range(2))
    head_turned = by_rows(by_head[:, 0].transpose(1, 2, 0))
    queries_turned = by_rows(query_proj.T)

    def operands(start, kv_head):
        q_rows = queries[start : start + stride, kv_head * group : (kv_head + 1) * group]
        key_span = extended[start : start + stride + WINDOW, kv_head * DH : (kv_head + 1) * DH]
        value_rows = extended[
            start : start + stride + WINDOW, (KVH + kv_head) * DH : (KVH + kv_head + 1) * DH
        ]
        return (q_rows, key_span, value_rows)

    def scores_of(q_rows, key_span, start):
        allowed = band_mask(first_row + start, stride)
        scores = (
            jnp.einsum("thd,jd->htj", q_rows, key_span, preferred_element_type=jnp.float32) * scale
        )
        return jnp.where(allowed[None], scores, NEG)

    start = 0
    head_outs = []
    span_stats = []
    for kv_head in range(KVH):
        q_rows, key_span, value_rows = operands(start, kv_head)
        scores = scores_of(q_rows, key_span, start)
        sinks = sink_logits[kv_head * group : (kv_head + 1) * group][:, None]
        peak = jnp.maximum(jnp.max(scores, axis=2), sinks)
        weights = jnp.exp(scores - peak[:, :, None])
        total = jnp.sum(weights, axis=2) + jnp.exp(sinks - peak)
        summed = jnp.einsum(
            "htj,jd->thd",
            weights.astype(jnp.bfloat16),
            value_rows,
            preferred_element_type=jnp.float32,
        )
        head_outs.append(summed / total.T[:, :, None])
        span_stats.append((peak, total))
    stats = [span_stats]
    out_rows = jnp.concatenate(head_outs, axis=1)
    attn = out_rows.reshape(tok_dev, HQ * DH).astype(jnp.bfloat16)
    targets = slot_targets(expert_ids, experts, capacity)
    slot_table = jnp.arange(experts * capacity, dtype=jnp.int32)
    picks = (targets[:, :, None] == slot_table[None, None, :]).astype(jnp.bfloat16)
    placed = jnp.sum(picks, axis=1)
    grad_f = out_grad.astype(jnp.float32)
    slot_weight = jnp.sum(gate_weights[:, :, None] * picks.astype(jnp.float32), axis=(0, 1))
    grad_slots = (slot_weight[:, None] * contract_rows(placed, out_grad)).astype(jnp.bfloat16)
    grad_slots = by_rows(grad_slots)
    over, up_over, down_over, grad_slots = lax.optimization_barrier(
        (over, up_over, down_over, grad_slots)
    )
    by_place = attn.reshape(tok_dev, 8, 2, 2 * DH)
    first, second = by_place[:, :, 0], by_place[:, :, 1]
    theirs = send(jnp.where(core == 0, second, first), TO_PEER).reshape(tok_dev, HQ * DH // 2)
    mine = jnp.where(core == 0, first, second).reshape(tok_dev, HQ * DH // 2)
    joined, for_peer, for_own = collect(
        where,
        (out_weight, above, below, across, up, down, over, up_over, down_over),
        jnp.concatenate([theirs.T, mine.T], axis=1),
    )
    attn_out = for_own.T + send(for_peer.T, TO_PEER)
    resid = lax.optimization_barrier(
        (hidden_in.astype(jnp.float32) + attn_out).astype(jnp.bfloat16)
    )
    resid = by_columns(resid)
    resid_f = resid.astype(jnp.float32)
    inv_rms = lax.rsqrt(jnp.mean(resid_f * resid_f, axis=1, keepdims=True) + EPS)
    normed = (resid_f * inv_rms * norm_gain).astype(jnp.bfloat16)
    def exchange(slots):
        return lax.all_to_all(
            slots.reshape(experts, capacity, D),
            AXES,
            split_axis=0,
            concat_axis=0,
            tiled=True,
            axis_index_groups=CORE_GROUPS,
        )

    def swap(value):
        return send(by_rows(value.reshape(experts, capacity, D)), TO_PEER)

    def flat(value):
        return by_rows(by_rows(value).reshape(experts * capacity, D))

    def add_halves(own, received):
        return (own.astype(jnp.float32) + received.astype(jnp.float32)).astype(jnp.bfloat16)

    w_gate = gate_proj[0]
    w_up = up_proj[0]
    w_down = down_proj[0]
    grads_own = exchange(grad_slots)
    grads_peer = flat(swap(grads_own))
    act_grad_own = by_columns(contract_cols(flat(grads_own), w_down))
    act_grad_peer = by_columns(contract_cols(grads_peer, w_down))

    slots_in = contract_rows(placed, normed).astype(jnp.bfloat16)
    early = (head_keys, head_values, head_turned, queries_turned, by_rows(resid), by_rows(out_grad))
    rows_own, act_grad_own, act_grad_peer, early = lax.optimization_barrier(
        (exchange(by_rows(slots_in)), act_grad_own, act_grad_peer, early)
    )
    head_keys, head_values, head_turned, queries_turned, resid_rows, grad_rows = early
    rows_peer = flat(swap(rows_own))
    rows_own = in_vmem(
        copy_body, jax.ShapeDtypeStruct((experts * capacity, D), jnp.bfloat16), flat(rows_own)
    )

    def hidden_units(rows, act_grad):
        gate_act = jnp.dot(rows, w_gate, preferred_element_type=jnp.float32)
        up_act = jnp.dot(rows, w_up, preferred_element_type=jnp.float32)
        sig = jax.nn.sigmoid(ALPHA * gate_act)
        act = (gate_act * sig * (up_act + 1.0)).astype(jnp.bfloat16)
        gate_grad = (
            act_grad * (up_act + 1.0) * sig * (1.0 + ALPHA * gate_act * (1.0 - sig))
        ).astype(jnp.bfloat16)
        up_grad = (act_grad * gate_act * sig).astype(jnp.bfloat16)
        return act, gate_grad, up_grad

    def row_grad_of(gate_grad, up_grad):
        return (contract_cols(gate_grad, w_gate) + contract_cols(up_grad, w_up)).astype(jnp.bfloat16)

    act_own, gate_grad_own, up_grad_own = hidden_units(rows_own, act_grad_own)
    rows_peer, act_own, gate_grad_own, up_grad_own = lax.optimization_barrier(
        (rows_peer, act_own, gate_grad_own, up_grad_own)
    )
    act_peer, gate_grad_peer, up_grad_peer = hidden_units(rows_peer, act_grad_peer)
    row_grad_peer = flat(swap(by_rows(row_grad_of(gate_grad_peer, up_grad_peer))))
    row_grad_own = lax.optimization_barrier(by_rows(row_grad_of(gate_grad_own, up_grad_own)))
    row_grad = by_rows(add_halves(row_grad_own, row_grad_peer))
    row_grad, act_own, act_peer = lax.optimization_barrier((row_grad, act_own, act_peer))
    normed_slots = flat(exchange(row_grad))
    rows_shape = jax.ShapeDtypeStruct((experts * capacity, D), jnp.bfloat16)
    part_peer = in_vmem(down_body, rows_shape, by_columns(act_peer).T, w_down)
    part_peer = by_rows(part_peer.reshape(experts, capacity, D))
    part_peer = [
        by_rows(by_rows(send(part, TO_PEER)).reshape(-1, D)) for part in jnp.split(part_peer, 4)
    ]
    part_sum = in_vmem(down_add_body, rows_shape, by_columns(act_own).T, w_down, *part_peer)
    expert_out = flat(exchange(part_sum))

    combine = jnp.sum(gate_weights[:, :, None] * picks.astype(jnp.float32), axis=1)
    combine_high = combine.astype(jnp.bfloat16)
    combine_low = (combine - combine_high.astype(jnp.float32)).astype(jnp.bfloat16)
    layer_out = in_vmem(
        mix_body,
        jax.ShapeDtypeStruct((D, tok_dev), jnp.bfloat16),
        combine_high,
        combine_low,
        expert_out,
        resid_rows,
    ).T
    resid_grad = in_vmem(
        resid_grad_body,
        jax.ShapeDtypeStruct((tok_dev, D), jnp.bfloat16),
        placed,
        normed_slots,
        resid_rows,
        grad_rows,
        inv_rms,
        norm_gain.reshape(1, D),
    )
    peer_grad = send(resid_grad.reshape(tok_dev // 8, 8, D), TO_PEER).reshape(tok_dev, D)

    def attn_grad_of(value):
        return in_vmem(
            attn_grad_body,
            jax.ShapeDtypeStruct((HQ * DH // 2, tok_dev), jnp.bfloat16),
            value,
            joined,
            scalars=where,
        ).reshape(8, 2 * DH, tok_dev)

    grad_mine = attn_grad_of(resid_grad)
    grad_back = send(attn_grad_of(peer_grad), TO_PEER)
    attn_grad = jnp.where(
        core == 0,
        jnp.stack([grad_mine, grad_back], axis=1),
        jnp.stack([grad_back, grad_mine], axis=1),
    ).reshape(HQ * DH, tok_dev)
    smem, vmem = (pl.BlockSpec(memory_space=space) for space in (pltpu.SMEM, pltpu.VMEM))
    query_grad, before, own = pl.pallas_call(
        attn_back_body,
        out_shape=[
            jax.ShapeDtypeStruct((tok_dev, HQ * DH), jnp.bfloat16),
            jax.ShapeDtypeStruct((WINDOW, 2 * KVH * DH), jnp.bfloat16),
            jax.ShapeDtypeStruct((tok_dev, 2 * KVH * DH), jnp.float32),
        ],
        in_specs=[smem, smem] + [vmem] * 5,
        out_specs=[vmem] * 3,
        compiler_params=pltpu.CompilerParams(vmem_limit_bytes=24 * 1024 * 1024),
        cost_estimate=pl.CostEstimate(flops=1000, bytes_accessed=1000, transcendentals=0),
    )(
        (device == 0).astype(jnp.int32).reshape(1),
        sink_logits,
        queries_turned,
        attn_grad,
        head_keys,
        head_turned,
        head_values,
    )
    returned = from_behind(before, ("ctx", "exp"), -1).astype(jnp.float32)
    own = own + returned
    key_grad = own[:, : KVH * DH].astype(jnp.bfloat16)
    value_grad = own[:, KVH * DH :].astype(jnp.bfloat16)
    return (layer_out, resid_grad, query_grad, key_grad, value_grad)


def solution(mesh):
    in_specs = (
        P(("ctx", "exp"), None),
        P(("ctx", "exp"), None),
        P(("ctx", "exp"), None),
        P(("ctx", "exp"), None),
        P(),
        P("exp", None),
        P(),
        P(("ctx", "exp"), None),
        P(("ctx", "exp"), None),
        P(("ctx", "exp"), None, None),
        P(("ctx", "exp"), None, None),
        P(("ctx", "exp"), None, None),
        P(("ctx", "exp"), None),
    )
    out_specs = (
        P(("ctx", "exp"), None),
        P(("ctx", "exp"), None),
        P(("ctx", "exp"), None),
        P(("ctx", "exp"), None),
        P(("ctx", "exp"), None),
    )
    return jax.shard_map(
        per_device, mesh=mesh, in_specs=in_specs, out_specs=out_specs, check_vma=False
    )
```
